32 devices in a mesh: az: 4 (over y, core), rad: 8 (over z, x).
Axes of the slice: x: 2, y: 2, z: 4, core: 2. Of those that a mesh axis runs over, the one named last changes fastest.
Arguments:
- state: float32 [8, 1, 256, 1024], P(None, None, 'rad', 'az'), may hold values from -6 to 6
- velocity: float32 [256], P('rad'), may hold values from -0.45 to 0.45
- coupling: float32 [8, 8], replicated, may hold values from -2 to 2
- diffusivity: float32 [8], replicated, may hold values from 1 to 4000, as said below
- inverse: float32 [8, 32, 32], replicated, as said below
- shifts: int32 [256], P('rad'), may hold values from 0 to 1023, as said below
Outputs:
- advected: float32 [8, 1, 256, 1024], P(None, None, 'rad', 'az')
The draws below stay inside these ranges and needn't reach their ends.
Inputs may be any that keep to these rules, and one draw needn't show every extreme that they name: `diffusivity`: one positive diffusion number a field, spread evenly in the logarithm. inverse[f] is, up to rounding, the inverse of the 32 x 32 tridiagonal matrix with 1 + 2 diffusivity[f] on the diagonal and -diffusivity[f] beside it. `shifts`: the shift falls with radius as in a Keplerian disc: from each row to the next it drops by 0 to 9 cells, modulo 1024.
All inputs are finite; a program needn't handle non-finite values.
Results may differ from the reference program's by a relative error of at most 0.00007.
Values sent between devices are 32-bit elements; how exact they have to be, the bound alone decides.
No kernel may reach another device: no remote copies, remote signals or barrier semaphores. Data moves between devices by JAX's collectives and lax.ppermute only.
A program may use at most 64 MiB of HBM per device.

```python
import jax
import jax.numpy as jnp
from jax import lax

FIELDS = 8
PLANES = 1
RAD_DEV = 32
NR = 256
NPHI = 1024
N_RAD = 8


def diffusion_numbers(key, low, high):
    unit = jax.random.uniform(key, (FIELDS,), jnp.float32)
    return jnp.exp(jnp.log(low) + unit * (jnp.log(high) - jnp.log(low)))


def block_inverse(numbers):
    ratio = jnp.sqrt(0.25 / numbers)
    theta = 2.0 * jnp.log(ratio + jnp.sqrt(0.25 / numbers + 1.0))
    rows = jnp.arange(RAD_DEV, dtype=jnp.float32) + 1.0
    lower = jnp.minimum(rows[:, None], rows[None, :])
    upper = jnp.maximum(rows[:, None], rows[None, :])
    angle = theta[:, None, None]
    numer = jnp.sinh(lower[None] * angle) * jnp.sinh((RAD_DEV + 1.0 - upper[None]) * angle)
    denom = numbers[:, None, None] * jnp.sinh(angle) * jnp.sinh((RAD_DEV + 1.0) * angle)
    return numer / denom


def draw_diffusivity(key, part):
    low, high = (2.0, 3000.0)
    return diffusion_numbers(key, low, high)


def draw_inverse(key, part):
    low, high = (2.0, 3000.0)
    return block_inverse(diffusion_numbers(key, low, high))


def draw_shifts(key, part):
    key = jax.random.fold_in(key, 7)
    key_inner, key_scale, key_jitter, key_pivot = jax.random.split(key, 4)
    inner_edge = jax.random.randint(key_inner, (), 64, 257, dtype=jnp.int32)
    rate_scale = jax.random.randint(key_scale, (), 2, 9, dtype=jnp.int32)
    row_ids = jnp.arange(NR, dtype=jnp.int32)
    radius = inner_edge + row_ids
    jitter = jax.random.randint(key_jitter, (NR,), 0, 2, dtype=jnp.int32)
    drops = jitter + rate_scale * inner_edge * inner_edge // (radius * radius)
    pivot_row = jax.random.randint(key_pivot, (), 1, NR - 1, dtype=jnp.int32)
    forced = (row_ids == pivot_row) | (row_ids == pivot_row + 1)
    drops = jnp.where(forced, jnp.int32(1), drops)
    climb = jnp.cumsum(drops).astype(jnp.int32)
    anchor = jnp.sum(jnp.where(row_ids == pivot_row, climb, jnp.int32(0)))
    return ((anchor - climb) % NPHI).astype(jnp.int32)


def level_of(rng, dims, cuts, least, high):
    def one(dim, parts):
        draws = jax.random.uniform(jax.random.fold_in(jax.random.fold_in(rng, 6), dim), (parts,), jnp.float32, least / len(cuts), high / len(cuts))
        return jnp.repeat(jnp.exp(draws), dims[dim] // parts).reshape((-1,) + (1,) * (len(dims) - dim - 1))

    loudness = one(*cuts[0])
    for cut in cuts[1:]:
        loudness = loudness * one(*cut)
    return loudness


def scatter_about(stream_key, dims, deviation, limit, cuts=(), kind=jnp.bfloat16):
    level = level_of(stream_key, dims, cuts, -0.22, 0.18) if cuts else 1.0
    result = jax.random.normal(stream_key, dims, jnp.float32) * deviation * level
    return jnp.minimum(jnp.maximum(result, -limit), limit).astype(kind)


def setup_inputs(seed: int = 0) -> dict:
    streams_of = jax.random.split(jax.random.key(seed), 7)
    return {
        "state": scatter_about(streams_of[0], (FIELDS, PLANES, NR, NPHI), 1.0, 6.0, ((2, 8), (3, 4)), jnp.float32),
        "velocity": jnp.clip(jax.random.uniform(streams_of[1], (NR,), jnp.float32, -0.45, 0.45) * level_of(streams_of[1], (NR,), ((0, 8),), -0.4, 0.0), -0.45, 0.45),
        "coupling": scatter_about(streams_of[2], (FIELDS, FIELDS), FIELDS ** -0.5, 2.0, (), jnp.float32),
        "diffusivity": draw_diffusivity(jax.random.fold_in(streams_of[6], 71), 0),
        "inverse": draw_inverse(jax.random.fold_in(streams_of[6], 71), 0),
        "shifts": draw_shifts(jax.random.fold_in(streams_of[6], 71), 0),
    }


highest = lax.Precision.HIGHEST


def flux_update(state, velocity, coupling):
    east = jnp.roll(state, -1, axis=3)
    west = jnp.roll(state, 1, axis=3)
    padded = jnp.pad(state, ((0, 0), (0, 0), (1, 1), (0, 0)))
    radial_diff = padded[:, :, 2:] - padded[:, :, :-2]
    mixed_terms = jnp.einsum("fg,gzrp->fzrp", coupling, radial_diff, precision=highest)
    return state - 0.5 * velocity[None, None, :, None] * (east - west) + 0.5 * mixed_terms


def chain_coefficients(diffusivity, inverse):
    last = inverse.shape[1] - 1
    return (diffusivity * inverse[:, 0, 0], diffusivity * inverse[:, last, 0],
            diffusivity * inverse[:, 0, last], diffusivity * inverse[:, last, last])


def pivot_chain(count, coeffs):
    first_first, last_first, first_last, last_last = coeffs

    def advance(pivot, unused):
        nxt = last_last + last_first * first_last * pivot / (1.0 - first_first * pivot)
        return nxt, pivot

    start_pivot = jnp.zeros_like(first_first)
    unused_end, pivots = lax.scan(advance, start_pivot, None, length=count)
    return pivots


def sweep_chain(heads, tails, coeffs, pivots):
    first_first, last_first, first_last, last_last = coeffs
    col = (slice(None), None, None)

    def forward(sweep_prev, items):
        head, tail, pivot = items
        quotient = 1.0 - first_first * pivot
        sweep_new = tail + (last_first * pivot / quotient)[col] * head + (last_first / quotient)[col] * sweep_prev
        return sweep_new, sweep_prev

    start_sweep = jnp.zeros_like(heads[0])
    unused_end, sweep_prevs = lax.scan(forward, start_sweep, (heads, tails, pivots))

    def backward(front_next, items):
        head, sweep_prev, pivot = items
        quotient = 1.0 - first_first * pivot
        front_now = (head + first_first[col] * sweep_prev) / quotient[col] + (first_last / quotient)[col] * front_next
        return front_now, front_next

    unused_first, front_nexts = lax.scan(backward, jnp.zeros_like(heads[0]), (heads, sweep_prevs, pivots), reverse=True)
    return sweep_prevs, front_nexts


def reference(state, velocity, coupling, diffusivity, inverse, shifts):
    fields_count, planes_count, rows_total, cells_total = state.shape
    block_rows = inverse.shape[1]
    updated = flux_update(state, velocity, coupling)
    blocks = updated.reshape(fields_count, planes_count, N_RAD, block_rows, cells_total)
    solved = jnp.einsum("frk,fzbkp->fzbrp", inverse, blocks, precision=highest)
    heads = jnp.moveaxis(solved[:, :, :, 0], 2, 0)
    tails = jnp.moveaxis(solved[:, :, :, block_rows - 1], 2, 0)
    coeffs = chain_coefficients(diffusivity, inverse)
    pivots = pivot_chain(N_RAD, coeffs)
    sweep_prevs, front_nexts = sweep_chain(heads, tails, coeffs, pivots)
    first_first, last_first, first_last, last_last = coeffs
    quotient = (1.0 - first_first[None, :] * pivots)[:, :, None, None]
    front_now = (heads + first_first[None, :, None, None] * sweep_prevs) / quotient + (first_last[None, :, None, None] / quotient) * front_nexts
    rear = sweep_prevs + pivots[:, :, None, None] * front_now
    rear_moved = jnp.moveaxis(rear, 0, 2)
    front_moved = jnp.moveaxis(front_nexts, 0, 2)
    first_column = inverse[:, :, 0][:, None, None, :, None]
    last_column = inverse[:, :, block_rows - 1][:, None, None, :, None]
    solution = solved + diffusivity[:, None, None, None, None] * (
        first_column * rear_moved[:, :, :, None, :] + last_column * front_moved[:, :, :, None, :])
    solution = solution.reshape(fields_count, planes_count, rows_total, cells_total)
    cells = jnp.arange(cells_total, dtype=jnp.int32)
    source = (cells[None, :] - shifts.astype(jnp.int32)[:, None]) % cells_total
    return jnp.take_along_axis(solution, jnp.broadcast_to(source, solution.shape), axis=3)
```

```python
import functools

import jax
import jax.numpy as jnp
from jax import lax
from jax.experimental import pallas as pl
from jax.experimental.pallas import tpu as pltpu
from jax.sharding import PartitionSpec as P

highest = lax.Precision.HIGHEST
LANES = 128


def swapped(block, axis, bit):
    return lax.ppermute(block, axis, [(i, i ^ bit) for i in range(lax.axis_size(axis))])


def local_solve(state, velocity, coupling, inverse):
    zero_row = jnp.zeros_like(state[:, :1])
    zero_col = jnp.zeros_like(state[:, :, :1])
    radial_diff = jnp.concatenate([state[:, 1:], zero_row], 1) - jnp.concatenate(
        [zero_row, state[:, :-1]], 1
    )
    east = jnp.concatenate([state[:, :, 1:], zero_col], 2)
    west = jnp.concatenate([zero_col, state[:, :, :-1]], 2)
    half = 0.5 * velocity[None, :, None]
    mixed = jnp.einsum("fg,grp->frp", coupling, radial_diff, precision=highest)
    updated = state - half * (east - west) + 0.5 * mixed
    ghosts = [half * state[:, :, -1:], -half * state[:, :, :1]]
    blank = jnp.zeros(state.shape[:2] + (LANES - 2,), state.dtype)
    wide = jnp.concatenate([updated] + ghosts + [blank], 2)
    return jnp.einsum("frk,fkp->frp", inverse, wide, precision=highest)


def chain(head, tail, coeffs):
    a, b, c, d = [x[:, None] for x in coeffs]
    place = lax.axis_index("rad")
    levels = []
    bit = 1
    while bit < lax.axis_size("rad"):
        other = swapped(jnp.stack([head, tail]), "rad", bit)
        upper = (place & bit) != 0
        q = 1.0 - a * d
        head_1 = jnp.where(upper, other[0], head)
        tail_1 = jnp.where(upper, other[1], tail)
        head_2 = jnp.where(upper, head, other[0])
        tail_2 = jnp.where(upper, tail, other[1])
        u = (head_2 + a * tail_1) / q
        w = (tail_1 + d * head_2) / q
        levels.append((upper, u, w, a * b / q, c / q, b / q, d * c / q))
        head, tail = head_1 + c * u, tail_2 + b * w
        a, b, c, d = a + a * b * c / q, b * b / q, c * c / q, d + b * c * d / q
        bit *= 2
    left = jnp.zeros_like(head)
    right = jnp.zeros_like(head)
    for upper, u, w, ul, ur, wl, wr in reversed(levels):
        inner_right = u + ul * left + ur * right
        inner_left = w + wl * left + wr * right
        left, right = jnp.where(upper, inner_left, left), jnp.where(upper, right, inner_right)
    return left, right


def finish_kernel(count, shifts_ref, place_ref, solved_ref, forcing_ref, columns_ref, out_ref):
    fields, rows, cells = out_ref.shape
    place = place_ref[0]
    lane = lax.broadcasted_iota(jnp.int32, (fields, cells), 1)
    for r in range(rows):
        hops = lax.div(shifts_ref[r], cells)
        residue = lax.rem(shifts_ref[r], cells)
        here = lax.rem(place - hops + count, count)
        before = lax.rem(here + count - 1, count)
        after = lax.rem(here + 1, count)
        source = here ^ place
        source_low = before ^ place
        source_high = jnp.where(residue > 0, here, after) ^ place
        own = lane < cells - residue
        left = jnp.where(own, forcing_ref[source, 0, :, :cells], forcing_ref[source_low, 0, :, :cells])
        right = jnp.where(own, forcing_ref[source, 1, :, :cells], forcing_ref[source_low, 1, :, :cells])
        first = columns_ref[0, :, r : r + 1]
        last = columns_ref[1, :, r : r + 1]
        low_l = forcing_ref[source_low, 0, :, cells:]
        low_r = forcing_ref[source_low, 1, :, cells:]
        high_l = forcing_ref[source_high, 0, :, cells:]
        high_r = forcing_ref[source_high, 1, :, cells:]
        low = low_l[:, 32 + r : 33 + r] + first * low_l[:, 0:1] + last * low_r[:, 0:1]
        high = high_r[:, 32 + r : 33 + r] + first * high_l[:, 1:2] + last * high_r[:, 1:2]
        value = solved_ref[:, r, :] + first * left + last * right
        value = value + jnp.where(lane == 0, low, 0.0) + jnp.where(lane == cells - 1, high, 0.0)
        out_ref[:, r, :] = pltpu.roll(value, residue, 1)


def per_device(state, velocity, coupling, diffusivity, inverse, shifts):
    state = state[:, 0]
    fields, rows, cells = state.shape
    count = lax.axis_size("az")
    place = lax.axis_index("az")
    solved = local_solve(state, velocity, coupling, inverse)
    edge_rows = jnp.stack([state[:, 0], state[:, -1]])
    edge_mix = 0.5 * jnp.einsum("fg,egp->efp", coupling, edge_rows, precision=highest)
    edge_mix = jnp.pad(edge_mix, ((0, 0), (0, 0), (0, LANES)))
    head = diffusivity[:, None] * solved[:, 0] + edge_mix[0]
    tail = diffusivity[:, None] * solved[:, -1] - edge_mix[1]
    coeffs = (
        diffusivity * inverse[:, 0, 0],
        diffusivity * inverse[:, -1, 0],
        diffusivity * inverse[:, 0, -1],
        diffusivity * inverse[:, -1, -1],
    )
    hops = (shifts // cells)[:, None] + (
        jnp.arange(cells, dtype=jnp.int32)[None] >= cells - (shifts % cells)[:, None]
    )
    crossing = (place - hops) ^ place
    moved = solved[:, :, :cells]
    bit = 1
    while bit < count:
        moved = jnp.where(((crossing & bit) != 0)[None], swapped(moved, "az", bit), moved)
        bit *= 2
    left, right = chain(head, tail, coeffs)
    ghosts = jnp.stack([solved[:, :, cells], solved[:, :, cells + 1]])
    forcing = jnp.stack([left, right])
    forcing = jnp.concatenate(
        [
            forcing[:, :, : cells + 32],
            ghosts,
            jnp.zeros((2, fields, LANES - 32 - rows), state.dtype),
        ],
        2,
    )[None]
    bit = 1
    while bit < count:
        forcing = jnp.concatenate([forcing, swapped(forcing, "az", bit)], 0)
        bit *= 2
    columns = jnp.stack([inverse[:, :, 0], inverse[:, :, -1]])
    out = pl.pallas_call(
        functools.partial(finish_kernel, count),
        out_shape=jax.ShapeDtypeStruct((fields, rows, cells), state.dtype),
        in_specs=[pl.BlockSpec(memory_space=pltpu.SMEM)] * 2
        + [pl.BlockSpec(memory_space=pltpu.VMEM)] * 3,
        out_specs=pl.BlockSpec(memory_space=pltpu.VMEM),
    )(shifts, place[None].astype(jnp.int32), moved, forcing, columns)
    return out[:, None]


def solution(mesh):
    return jax.shard_map(
        per_device,
        mesh=mesh,
        in_specs=(P(None, None, "rad", "az"), P("rad"), P(), P(), P(), P("rad")),
        out_specs=P(None, None, "rad", "az"),
        check_vma=False,
    )
```

```python
import functools

import jax
import jax.numpy as jnp
from jax import lax
from jax.experimental import pallas as pl
from jax.experimental.pallas import tpu as pltpu
from jax.sharding import PartitionSpec as P

highest = lax.Precision.HIGHEST
f32 = jnp.float32
LANES = 128
SMEM = pl.BlockSpec(memory_space=pltpu.SMEM)
VMEM = pl.BlockSpec(memory_space=pltpu.VMEM)
ANY = pl.BlockSpec(memory_space=pl.ANY)


def in_vmem(x):
    return pltpu.with_memory_space_constraint(x, pltpu.VMEM)


def iota(shape, dim):
    return lax.broadcasted_iota(jnp.int32, shape, dim)


def log2(number):
    assert number & (number - 1) == 0
    return number.bit_length() - 1


def swapped(block, axis, bit):
    return lax.ppermute(block, axis, [(i, i ^ bit) for i in range(lax.axis_size(axis))])


def tile(x, j):
    return x[:, j * LANES : (j + 1) * LANES]


def as_column(row):
    n = row.shape[1]
    same = iota((n, n), 0) == iota((n, n), 1)
    return jnp.sum(jnp.where(same, jnp.broadcast_to(row, (n, n)), 0.0), axis=1, keepdims=True)


def level_coefficients(first, last, count, place):
    fields = first.shape[0]
    wide = (fields, LANES)
    a = jnp.broadcast_to(first[:, :1], wide)
    b = jnp.broadcast_to(last[:, :1], wide)
    c = jnp.broadcast_to(first[:, -1:], wide)
    d = jnp.broadcast_to(last[:, -1:], wide)
    one, none = jnp.ones(wide, f32), jnp.zeros(wide, f32)
    left_l, left_r, right_l, right_r = one, none, none, one
    found = []
    bit = 1
    while bit < count:
        side = iota(wide, 0) * 0 + (place & bit)
        upper = side != 0
        q = 1.0 / (1.0 - a * d)
        own = q * jnp.where(upper, d, a)
        felt_l = jnp.where(upper, left_l, left_r)
        felt_r = jnp.where(upper, right_l, right_r)
        if 2 * bit == count:
            found += [felt_l * q, felt_l * own, felt_r * q, felt_r * own]
            break
        found += [q, own, q * jnp.where(upper, a, d), felt_l, felt_r, b, c]
        via_l = jnp.where(upper, b * q, a * b * q)
        via_r = jnp.where(upper, c * d * q, c * q)
        left_l, left_r = (
            jnp.where(upper, none, left_l) + felt_l * via_l,
            jnp.where(upper, left_r, none) + felt_l * via_r,
        )
        right_l, right_r = (
            jnp.where(upper, none, right_l) + felt_r * via_l,
            jnp.where(upper, right_r, none) + felt_r * via_r,
        )
        a, b, c, d = a + a * b * c * q, b * b * q, c * c * q, d + b * c * d * q
        bit *= 2
    return found


def offsets_kernel(
    count, state_hbm, inverse_hbm, velocity_hbm, coupling_hbm, diffusivity_hbm,
    out_ref, coeffs_ref, state_ref, inverse_ref, velocity_ref, coupling_ref, diffusivity_ref, sems,
):
    copies = [
        pltpu.make_async_copy(source, target, sems.at[i])
        for i, (source, target) in enumerate(
            (
                (inverse_hbm, inverse_ref),
                (velocity_hbm, velocity_ref),
                (coupling_hbm, coupling_ref),
                (diffusivity_hbm, diffusivity_ref),
                (state_hbm, state_ref),
            )
        )
    ]
    for copy in copies:
        copy.start()
    for copy in copies[:4]:
        copy.wait()
    fields, rows, cells = state_ref.shape
    span = fields * rows
    diffusivity = as_column(diffusivity_ref[...])
    first = diffusivity * inverse_ref[:, 0, :]
    last = diffusivity * inverse_ref[:, rows - 1, :]
    for i, x in enumerate(level_coefficients(first, last, count, lax.axis_index("rad"))):
        coeffs_ref[i] = x
    first = jnp.concatenate([first] * fields, axis=1)
    last = jnp.concatenate([last] * fields, axis=1)
    speed = jnp.concatenate([jnp.broadcast_to(velocity_ref[...], (fields, rows))] * fields, axis=1)
    lane = iota((fields, span), 1)
    row = lane & (rows - 1)
    group = lane >> log2(rows)
    own = group == iota((fields, span), 0)
    mix = jnp.zeros((fields, span), f32)
    for g in range(fields):
        mix = jnp.where(group == g, coupling_ref[:, g : g + 1], mix)
    weights = []
    drift = []
    for vector, below, above in ((first, 1.0, 0.0), (last, 0.0, 1.0)):
        lower = jnp.where(row == 0, below, pltpu.roll(vector, 1, 1))
        upper = jnp.where(row == rows - 1, above, pltpu.roll(vector, span - 1, 1))
        weights.append(jnp.where(own, vector, 0.0) + 0.5 * mix * (lower - upper))
        drift.append(jnp.where(own, 0.5 * speed * vector, 0.0))
    table = jnp.concatenate(weights + drift, axis=0)
    copies[4].wait()
    sums = jnp.dot(
        table,
        state_ref[...].reshape(span, cells),
        precision=highest,
        preferred_element_type=f32,
    )
    blank = jnp.zeros((2 * fields, LANES), f32)
    main = jnp.concatenate([sums[: 2 * fields], blank], axis=1)
    side = jnp.concatenate([sums[2 * fields :], blank], axis=1)
    width = cells + LANES
    total = main + pltpu.roll(side, 1, 1) - pltpu.roll(side, width - 1, 1)
    for e in range(2):
        for j in range(width // LANES):
            out_ref[e, j] = tile(total[e * fields : (e + 1) * fields], j)


def solve_kernel(
    count, coupling_ref, state_ref, velocity_ref, inverse_ref,
    out_ref, columns_ref, diff_ref, updated_ref, table_ref,
):
    fields, rows, cells = state_ref.shape
    span = fields * rows
    width = cells + LANES
    row = iota((rows, cells), 0)
    half = 0.5 * as_column(velocity_ref[...])
    for g in range(fields):
        block = state_ref[g]
        upper = jnp.where(row == rows - 1, 0.0, pltpu.roll(block, rows - 1, 0))
        lower = jnp.where(row == 0, 0.0, pltpu.roll(block, 1, 0))
        diff_ref[g] = 0.5 * (upper - lower)
        padded = jnp.concatenate([block, jnp.zeros((rows, LANES), f32)], axis=1)
        updated_ref[g * rows : (g + 1) * rows] = padded + half * (
            pltpu.roll(padded, 1, 1) - pltpu.roll(padded, width - 1, 1)
        )
        pad = [jnp.zeros((rows, rows), f32)] * fields
        pad[g] = inverse_ref[g]
        placed = jnp.concatenate(pad, axis=1)
        for j in range(span // LANES):
            table_ref[j, pl.ds(g, rows, stride=fields), :] = tile(placed, j)
    for f in range(fields):
        total = updated_ref[f * rows : (f + 1) * rows, :cells]
        for g in range(fields):
            total = total + coupling_ref[f, g] * diff_ref[g]
        updated_ref[f * rows : (f + 1) * rows, :cells] = total
    solved = jnp.dot(
        jnp.concatenate([table_ref[j] for j in range(span // LANES)], axis=1),
        updated_ref[...],
        precision=highest,
        preferred_element_type=f32,
    )
    lane = iota((fields, LANES), 1)
    ghosts = jnp.zeros((fields, LANES), f32)
    for r in range(rows):
        block = solved[r * fields : (r + 1) * fields]
        out_ref[r, 0] = tile(block, 0)
        out_ref[r, 1] = tile(block, 1)
        edge = tile(block, 2)
        ghosts = jnp.where(lane == r, pltpu.roll(edge, r, 1), ghosts)
        ghosts = jnp.where(lane == rows + r, pltpu.roll(edge, rows + r + 1, 1), ghosts)
        columns_ref[0, r] = jnp.broadcast_to(inverse_ref[:, r, :1], (fields, LANES))
        columns_ref[1, r] = jnp.broadcast_to(inverse_ref[:, r, rows - 1 :], (fields, LANES))
    place = lax.axis_index("az")
    for at in range(count * 2 * rows // LANES):
        for part in range(LANES // (2 * rows)):
            mine = iota((fields, LANES), 0) * 0 + place == at * (LANES // (2 * rows)) + part
            moved = pltpu.roll(ghosts, part * 2 * rows, 1) if part else ghosts
            value = jnp.where(mine, moved, 0.0)
            total = value if part == 0 else total + value
        out_ref[rows + at // 2, at % 2] = total


def masks(shift, cells, place, bit):
    hops = shift >> log2(cells)
    residue = shift & (cells - 1)
    near = ((place - hops) ^ place) & bit
    far = ((place - hops - 1) ^ place) & bit
    lane = iota((8, LANES), 1)
    return [jnp.where(lane + j * LANES < cells - residue, near, far) != 0 for j in range(2)]


def select_kernel(bit, shifts_ref, kept_ref, came_ref, out_ref):
    rows = shifts_ref.shape[0]
    place = lax.axis_index("az")
    for r in range(rows):
        take = masks(shifts_ref[r], 2 * LANES, place, bit)
        for j in range(2):
            out_ref[r, j] = jnp.where(take[j], came_ref[r, j], kept_ref[r, j])
    out_ref[rows:] = kept_ref[rows:] + came_ref[rows:]


def turned(value, residue):
    amount = residue & (LANES - 1)
    low = iota(value[0].shape, 1) < amount
    turn = [pltpu.roll(x, amount, 1) for x in value]
    return [jnp.where(low, turn[1], turn[0]), jnp.where(low, turn[0], turn[1])]


def rotate_kernel(count, bit, shifts_ref, kept_ref, came_ref, out_ref, ghosts_ref):
    rows, tiles, fields, lanes = out_ref.shape
    cells = tiles * lanes
    per_tile = lanes // (2 * rows)
    place = lax.axis_index("az")
    lane = iota((fields, lanes), 1)
    for at in range(count * 2 * rows // lanes):
        ghosts_ref[at] = kept_ref[rows + at // 2, at % 2] + came_ref[rows + at // 2, at % 2]
    for r in range(rows):
        shift = shifts_ref[r]
        hops = shift >> log2(cells)
        residue = shift & (cells - 1)
        take = masks(shift, cells, place, bit)
        value = [jnp.where(take[j], came_ref[r, j], kept_ref[r, j]) for j in range(2)]
        here = (place - hops) & (count - 1)
        before = (here - 1) & (count - 1)
        after = jnp.where(residue > 0, here, (here + 1) & (count - 1))
        low_at = (before & (per_tile - 1)) * 2 * rows + r
        high_at = (after & (per_tile - 1)) * 2 * rows + rows + r
        low = pltpu.roll(ghosts_ref[before >> log2(per_tile)], (lanes - low_at) & (lanes - 1), 1)
        high = pltpu.roll(ghosts_ref[after >> log2(per_tile)], lanes - 1 - high_at, 1)
        value[0] = value[0] + jnp.where(lane == 0, low, 0.0)
        value[1] = value[1] + jnp.where(lane == lanes - 1, high, 0.0)
        value = turned(value, residue)
        swap = residue >> log2(lanes)
        out_ref[r, swap] = value[0]
        out_ref[r, 1 - swap] = value[1]


def finish_kernel(count, parts, shifts_ref, columns_ref, rotated_ref, *rest):
    out_hbm, forcing_ref, total_ref, sems = rest[parts:]
    rows, tiles, fields, lanes = rotated_ref.shape
    cells = tiles * lanes
    chunk = 8
    at = 0
    place = lax.axis_index("az")
    lane = iota((fields, lanes), 1)
    for part in rest[:parts]:
        forcing_ref[at : at + part.shape[0]] = part[...]
        at += part.shape[0]
    for m in range(count):
        before = (((place ^ m) - 1) & (count - 1)) ^ place
        after = (((place ^ m) + 1) & (count - 1)) ^ place
        for e in range(2):
            forcing_ref[m, e, 0] += jnp.where(lane == 0, forcing_ref[before, e, tiles], 0.0)
            forcing_ref[m, e, 1] += jnp.where(lane == lanes - 1, forcing_ref[after, e, tiles], 0.0)
    copies = []
    for r in range(rows):
        shift = shifts_ref[r]
        hops = shift >> log2(cells)
        residue = shift & (cells - 1)
        here = (place - hops) & (count - 1)
        source = here ^ place
        source_low = ((here - 1) & (count - 1)) ^ place
        value = []
        for j in range(2):
            near = lane + j * lanes < cells - residue
            left = jnp.where(near, forcing_ref[source, 0, j], forcing_ref[source_low, 0, j])
            right = jnp.where(near, forcing_ref[source, 1, j], forcing_ref[source_low, 1, j])
            value.append(columns_ref[0, r] * left + columns_ref[1, r] * right)
        value = turned(value, residue)
        swap = residue >> log2(lanes)
        for j, x in ((swap, value[0]), (1 - swap, value[1])):
            total_ref[r // chunk, j, pl.ds(r % chunk, fields, stride=chunk), :] = x + rotated_ref[r, j]
        if r % chunk == chunk - 1:
            for j in range(2):
                copies.append(
                    pltpu.make_async_copy(
                        total_ref.at[r // chunk, j].reshape(fields, chunk, lanes),
                        out_hbm.at[:, pl.ds(r + 1 - chunk, chunk), pl.ds(j * lanes, lanes)],
                        sems.at[r // chunk, j],
                    )
                )
                copies[-1].start()
    for copy in copies:
        copy.wait()


def chain(offsets, coeffs):
    place = lax.axis_index("rad")
    count = lax.axis_size("rad")
    head, tail = offsets[0], offsets[1]
    left = right = None
    bit = 1
    at = 0
    while 2 * bit < count:
        upper = (place & bit) != 0
        q, own, other_scale, felt_l, felt_r, b, c = [coeffs[at + i] for i in range(7)]
        at += 7
        other = swapped(jnp.stack([head, tail]), "rad", bit)
        meeting = jnp.where(upper, other[1], other[0])
        facing = jnp.where(upper, head, tail)
        inner = q * meeting + own * facing
        partner = q * facing + other_scale * meeting
        left = felt_l * inner if left is None else left + felt_l * inner
        right = felt_r * inner if right is None else right + felt_r * inner
        head = jnp.where(upper, other[0], head) + c * jnp.where(upper, partner, inner)
        tail = jnp.where(upper, tail, other[1]) + b * jnp.where(upper, inner, partner)
        bit *= 2
    upper = (place & bit) != 0
    facing = jnp.where(upper, head, tail)
    meeting = swapped(facing, "rad", bit)
    return jnp.stack(
        [
            left + coeffs[at] * meeting + coeffs[at + 1] * facing,
            right + coeffs[at + 2] * meeting + coeffs[at + 3] * facing,
        ]
    )


def per_device(state, velocity, coupling, diffusivity, inverse, shifts):
    state = state[:, 0]
    fields, rows, cells = state.shape
    tiles = cells // LANES
    assert tiles == 2 and fields == 8 and 2 * rows <= LANES
    count = lax.axis_size("az")
    levels = log2(lax.axis_size("rad"))
    offsets, coeffs, state_near, inverse_near = pl.pallas_call(
        functools.partial(offsets_kernel, lax.axis_size("rad")),
        out_shape=[
            pltpu.VMEM((2, tiles + 1, fields, LANES), f32),
            pltpu.VMEM((7 * levels - 3, fields, LANES), f32),
            pltpu.VMEM(state.shape, f32),
            pltpu.VMEM(inverse.shape, f32),
        ],
        in_specs=[ANY] * 5,
        out_specs=[VMEM] * 4,
        scratch_shapes=[
            pltpu.VMEM((1, rows), f32),
            pltpu.VMEM((fields, fields), f32),
            pltpu.VMEM((1, fields), f32),
            pltpu.SemaphoreType.DMA((5,)),
        ],
        name="offsets",
    )(state, inverse, velocity[None], coupling, diffusivity[None])
    spare = count * 2 * rows // cells
    solved, columns = pl.pallas_call(
        functools.partial(solve_kernel, count),
        out_shape=[
            pltpu.VMEM((rows + spare, tiles, fields, LANES), f32),
            pltpu.VMEM((2, rows, fields, LANES), f32),
        ],
        in_specs=[SMEM] + [VMEM] * 3,
        out_specs=[VMEM] * 2,
        scratch_shapes=[
            pltpu.VMEM((fields, rows, cells), f32),
            pltpu.VMEM((fields * rows, cells + LANES), f32),
            pltpu.VMEM((fields * rows // LANES, fields * rows, LANES), f32),
        ],
        name="solve",
    )(coupling, in_vmem(state_near), velocity[None], in_vmem(inverse_near))
    kept = solved
    bit = 1
    while 2 * bit < count:
        kept = pl.pallas_call(
            functools.partial(select_kernel, bit),
            out_shape=pltpu.VMEM(solved.shape, f32),
            in_specs=[SMEM] + [VMEM] * 2,
            out_specs=VMEM,
            name="select",
        )(shifts, in_vmem(kept), in_vmem(swapped(kept, "az", bit)))
        bit *= 2
    rotated = pl.pallas_call(
        functools.partial(rotate_kernel, count, bit),
        out_shape=pltpu.VMEM((rows, tiles, fields, LANES), f32),
        in_specs=[SMEM] + [VMEM] * 2,
        out_specs=VMEM,
        scratch_shapes=[pltpu.VMEM((count * 2 * rows // LANES, fields, LANES), f32)],
        name="rotate",
    )(shifts, in_vmem(kept), in_vmem(swapped(kept, "az", bit)))
    forcing = chain(offsets, coeffs)
    parts = [forcing[None]]
    bit = 1
    while bit < count:
        parts.append(swapped(jnp.concatenate(parts, 0), "az", bit))
        bit *= 2
    out = pl.pallas_call(
        functools.partial(finish_kernel, count, len(parts)),
        out_shape=jax.ShapeDtypeStruct(state.shape, f32),
        in_specs=[SMEM] + [VMEM] * (2 + len(parts)),
        out_specs=ANY,
        scratch_shapes=[
            pltpu.VMEM((count, 2, tiles + 1, fields, LANES), f32),
            pltpu.VMEM((rows // 8, tiles, 8 * fields, LANES), f32),
            pltpu.SemaphoreType.DMA((rows // 8, tiles)),
        ],
        name="finish",
    )(shifts, in_vmem(columns), in_vmem(rotated), *map(in_vmem, parts))
    return out[:, None]


def solution(mesh):
    return jax.shard_map(
        per_device,
        mesh=mesh,
        in_specs=(P(None, None, "rad", "az"), P("rad"), P(), P(), P(), P("rad")),
        out_specs=P(None, None, "rad", "az"),
        check_vma=False,
    )
```

```python
import functools

import jax
import jax.numpy as jnp
from jax import lax
from jax.experimental import pallas as pl
from jax.experimental.pallas import tpu as pltpu
from jax.sharding import PartitionSpec as P

highest = lax.Precision.HIGHEST
f32 = jnp.float32
LANES = 128
SMEM = pl.BlockSpec(memory_space=pltpu.SMEM)
VMEM = pl.BlockSpec(memory_space=pltpu.VMEM)
ANY = pl.BlockSpec(memory_space=pl.ANY)


def cost(kilobytes):
    return pl.CostEstimate(flops=kilobytes << 18, bytes_accessed=kilobytes << 10, transcendentals=0)


def in_vmem(x):
    return pltpu.with_memory_space_constraint(x, pltpu.VMEM)


def iota(shape, dim):
    return lax.broadcasted_iota(jnp.int32, shape, dim)


def log2(number):
    assert number & (number - 1) == 0
    return number.bit_length() - 1


def swapped(block, axis, bit):
    return lax.ppermute(block, axis, [(i, i ^ bit) for i in range(lax.axis_size(axis))])


def tile(x, j):
    return x[:, j * LANES : (j + 1) * LANES]


def as_column(row):
    n = row.shape[1]
    same = iota((n, n), 0) == iota((n, n), 1)
    return jnp.sum(jnp.where(same, jnp.broadcast_to(row, (n, n)), 0.0), axis=1, keepdims=True)


def level_coefficients(first, last, count, place):
    fields = first.shape[0]
    wide = (fields, LANES)
    a = jnp.broadcast_to(first[:, :1], wide)
    b = jnp.broadcast_to(last[:, :1], wide)
    c = jnp.broadcast_to(first[:, -1:], wide)
    d = jnp.broadcast_to(last[:, -1:], wide)
    one, none = jnp.ones(wide, f32), jnp.zeros(wide, f32)
    left_l, left_r, right_l, right_r = one, none, none, one
    found = []
    bit = 1
    while bit < count:
        side = iota(wide, 0) * 0 + (place & bit)
        upper = side != 0
        q = 1.0 / (1.0 - a * d)
        own = q * jnp.where(upper, d, a)
        felt_l = jnp.where(upper, left_l, left_r)
        felt_r = jnp.where(upper, right_l, right_r)
        if 2 * bit == count:
            found += [felt_l * q, felt_l * own, felt_r * q, felt_r * own]
            break
        found += [q, own, q * jnp.where(upper, a, d), felt_l, felt_r, b, c]
        via_l = jnp.where(upper, b * q, a * b * q)
        via_r = jnp.where(upper, c * d * q, c * q)
        left_l, left_r = (
            jnp.where(upper, none, left_l) + felt_l * via_l,
            jnp.where(upper, left_r, none) + felt_l * via_r,
        )
        right_l, right_r = (
            jnp.where(upper, none, right_l) + felt_r * via_l,
            jnp.where(upper, right_r, none) + felt_r * via_r,
        )
        a, b, c, d = a + a * b * c * q, b * b * q, c * c * q, d + b * c * d * q
        bit *= 2
    return found


def offsets_kernel(
    state_hbm, inverse_hbm, velocity_hbm, coupling_hbm, diffusivity_hbm,
    out_ref, state_ref, inverse_ref, velocity_ref, coupling_ref, diffusivity_ref, sems,
):
    copies = [
        pltpu.make_async_copy(source, target, sems.at[i])
        for i, (source, target) in enumerate(
            (
                (inverse_hbm, inverse_ref),
                (velocity_hbm, velocity_ref),
                (coupling_hbm, coupling_ref),
                (diffusivity_hbm, diffusivity_ref),
                (state_hbm, state_ref),
            )
        )
    ]
    for copy in copies:
        copy.start()
    for copy in copies[:4]:
        copy.wait()
    fields, rows, cells = state_ref.shape
    span = fields * rows
    diffusivity = as_column(diffusivity_ref[...])
    first = diffusivity * inverse_ref[:, 0, :]
    last = diffusivity * inverse_ref[:, rows - 1, :]
    first = jnp.concatenate([first] * fields, axis=1)
    last = jnp.concatenate([last] * fields, axis=1)
    speed = jnp.concatenate([jnp.broadcast_to(velocity_ref[...], (fields, rows))] * fields, axis=1)
    lane = iota((fields, span), 1)
    row = lane & (rows - 1)
    group = lane >> log2(rows)
    own = group == iota((fields, span), 0)
    mix = jnp.zeros((fields, span), f32)
    for g in range(fields):
        mix = jnp.where(group == g, coupling_ref[:, g : g + 1], mix)
    weights = []
    drift = []
    for vector, below, above in ((first, 1.0, 0.0), (last, 0.0, 1.0)):
        lower = jnp.where(row == 0, below, pltpu.roll(vector, 1, 1))
        upper = jnp.where(row == rows - 1, above, pltpu.roll(vector, span - 1, 1))
        weights.append(jnp.where(own, vector, 0.0) + 0.5 * mix * (lower - upper))
        drift.append(jnp.where(own, 0.5 * speed * vector, 0.0))
    table = jnp.concatenate(weights + drift, axis=0)
    copies[4].wait()
    sums = jnp.dot(
        table,
        state_ref[...].reshape(span, cells),
        precision=highest,
        preferred_element_type=f32,
    )
    blank = jnp.zeros((2 * fields, LANES), f32)
    main = jnp.concatenate([sums[: 2 * fields], blank], axis=1)
    side = jnp.concatenate([sums[2 * fields :], blank], axis=1)
    width = cells + LANES
    total = main + pltpu.roll(side, 1, 1) - pltpu.roll(side, width - 1, 1)
    for e in range(2):
        for j in range(width // LANES):
            out_ref[e, j] = tile(total[e * fields : (e + 1) * fields], j)


def solve_kernel(
    count, segments, coupling_ref, state_ref, velocity_ref, diffusivity_ref, inverse_ref,
    out_ref, columns_ref, coeffs_ref, final_ref, diff_ref, updated_ref, table_ref,
):
    fields, rows, cells = state_ref.shape
    span = fields * rows
    width = cells + LANES
    row = iota((rows, cells), 0)
    half = 0.5 * as_column(velocity_ref[...])
    diffusivity = as_column(diffusivity_ref[...])
    first = diffusivity * inverse_ref[:, 0, :]
    last = diffusivity * inverse_ref[:, rows - 1, :]
    for i, x in enumerate(level_coefficients(first, last, segments, lax.axis_index("rad"))):
        if i < coeffs_ref.shape[0]:
            coeffs_ref[i] = x
        else:
            final_ref[i - coeffs_ref.shape[0]] = x
    for g in range(fields):
        block = state_ref[g]
        upper = jnp.where(row == rows - 1, 0.0, pltpu.roll(block, rows - 1, 0))
        lower = jnp.where(row == 0, 0.0, pltpu.roll(block, 1, 0))
        diff_ref[g] = 0.5 * (upper - lower)
        padded = jnp.concatenate([block, jnp.zeros((rows, LANES), f32)], axis=1)
        updated_ref[g * rows : (g + 1) * rows] = padded + half * (
            pltpu.roll(padded, 1, 1) - pltpu.roll(padded, width - 1, 1)
        )
        pad = [jnp.zeros((rows, rows), f32)] * fields
        pad[g] = inverse_ref[g]
        placed = jnp.concatenate(pad, axis=1)
        for j in range(span // LANES):
            table_ref[j, pl.ds(g, rows, stride=fields), :] = tile(placed, j)
    for f in range(fields):
        total = updated_ref[f * rows : (f + 1) * rows, :cells]
        for g in range(fields):
            total = total + coupling_ref[f, g] * diff_ref[g]
        updated_ref[f * rows : (f + 1) * rows, :cells] = total
    solved = jnp.dot(
        jnp.concatenate([table_ref[j] for j in range(span // LANES)], axis=1),
        updated_ref[...],
        precision=highest,
        preferred_element_type=f32,
    )
    lane = iota((fields, LANES), 1)
    ghosts = jnp.zeros((fields, LANES), f32)
    for r in range(rows):
        block = solved[r * fields : (r + 1) * fields]
        out_ref[r, 0] = tile(block, 0)
        out_ref[r, 1] = tile(block, 1)
        edge = tile(block, 2)
        ghosts = jnp.where(lane == r, pltpu.roll(edge, r, 1), ghosts)
        ghosts = jnp.where(lane == rows + r, pltpu.roll(edge, rows + r + 1, 1), ghosts)
        columns_ref[0, r] = jnp.broadcast_to(inverse_ref[:, r, :1], (fields, LANES))
        columns_ref[1, r] = jnp.broadcast_to(inverse_ref[:, r, rows - 1 :], (fields, LANES))
    place = lax.axis_index("az")
    for at in range(count * 2 * rows // LANES):
        for part in range(LANES // (2 * rows)):
            mine = iota((fields, LANES), 0) * 0 + place == at * (LANES // (2 * rows)) + part
            moved = pltpu.roll(ghosts, part * 2 * rows, 1) if part else ghosts
            value = jnp.where(mine, moved, 0.0)
            total = value if part == 0 else total + value
        out_ref[rows + at // 2, at % 2] = total


def masks(shift, cells, place, bit):
    residue = shift & (cells - 1)
    hops = shift >> log2(cells)
    near = ((place - hops) ^ place) & bit
    far = ((place - hops - 1) ^ place) & bit
    lane = iota((8, LANES), 1)
    return [jnp.where(lane + j * LANES < cells - residue, near, far) != 0 for j in range(2)]


def select_kernel(bit, shifts_ref, kept_ref, came_ref, coeffs_ref, out_ref, later_ref):
    later_ref[...] = coeffs_ref[...]
    rows = shifts_ref.shape[0]
    place = lax.axis_index("az")
    for r in range(rows):
        take = masks(shifts_ref[r], 2 * LANES, place, bit)
        for j in range(2):
            out_ref[r, j] = jnp.where(take[j], came_ref[r, j], kept_ref[r, j])
    out_ref[rows:] = kept_ref[rows:] + came_ref[rows:]


def turned(value, residue):
    amount = residue & (LANES - 1)
    low = iota(value[0].shape, 1) < amount
    turn = [pltpu.roll(x, amount, 1) for x in value]
    return [jnp.where(low, turn[1], turn[0]), jnp.where(low, turn[0], turn[1])]


def rotate_kernel(count, bit, shifts_ref, kept_ref, came_ref, out_ref, ghosts_ref):
    rows, tiles, fields, lanes = out_ref.shape
    cells = tiles * lanes
    per_tile = lanes // (2 * rows)
    place = lax.axis_index("az")
    lane = iota((fields, lanes), 1)
    for at in range(count * 2 * rows // lanes):
        ghosts_ref[at] = kept_ref[rows + at // 2, at % 2] + came_ref[rows + at // 2, at % 2]
    for r in range(rows):
        shift = shifts_ref[r]
        hops = shift >> log2(cells)
        residue = shift & (cells - 1)
        take = masks(shift, cells, place, bit)
        value = [jnp.where(take[j], came_ref[r, j], kept_ref[r, j]) for j in range(2)]
        here = (place - hops) & (count - 1)
        before = (here - 1) & (count - 1)
        after = jnp.where(residue > 0, here, (here + 1) & (count - 1))
        low_at = (before & (per_tile - 1)) * 2 * rows + r
        high_at = (after & (per_tile - 1)) * 2 * rows + rows + r
        low = pltpu.roll(ghosts_ref[before >> log2(per_tile)], (lanes - low_at) & (lanes - 1), 1)
        high = pltpu.roll(ghosts_ref[after >> log2(per_tile)], lanes - 1 - high_at, 1)
        value[0] = value[0] + jnp.where(lane == 0, low, 0.0)
        value[1] = value[1] + jnp.where(lane == lanes - 1, high, 0.0)
        value = turned(value, residue)
        swap = residue >> log2(lanes)
        out_ref[r, swap] = value[0]
        out_ref[r, 1 - swap] = value[1]


def finish_kernel(count, parts, shifts_ref, columns_ref, rotated_ref, *rest):
    out_hbm, forcing_ref, total_ref, sems = rest[parts:]
    rows, tiles, fields, lanes = rotated_ref.shape
    cells = tiles * lanes
    chunk = 8
    at = 0
    place = lax.axis_index("az")
    lane = iota((fields, lanes), 1)
    for part in rest[:parts]:
        forcing_ref[at : at + part.shape[0]] = part[...]
        at += part.shape[0]
    for m in range(count):
        before = (((place ^ m) - 1) & (count - 1)) ^ place
        after = (((place ^ m) + 1) & (count - 1)) ^ place
        for e in range(2):
            forcing_ref[m, e, 0] += jnp.where(lane == 0, forcing_ref[before, e, tiles], 0.0)
            forcing_ref[m, e, 1] += jnp.where(lane == lanes - 1, forcing_ref[after, e, tiles], 0.0)
    copies = []
    for r in range(rows):
        shift = shifts_ref[r]
        hops = shift >> log2(cells)
        residue = shift & (cells - 1)
        here = (place - hops) & (count - 1)
        source = here ^ place
        source_low = ((here - 1) & (count - 1)) ^ place
        value = []
        for j in range(2):
            near = lane + j * lanes < cells - residue
            left = jnp.where(near, forcing_ref[source, 0, j], forcing_ref[source_low, 0, j])
            right = jnp.where(near, forcing_ref[source, 1, j], forcing_ref[source_low, 1, j])
            value.append(columns_ref[0, r] * left + columns_ref[1, r] * right)
        value = turned(value, residue)
        swap = residue >> log2(lanes)
        for j, x in ((swap, value[0]), (1 - swap, value[1])):
            total_ref[r // chunk, j, pl.ds(r % chunk, fields, stride=chunk), :] = x + rotated_ref[r, j]
        if r % chunk == chunk - 1:
            for j in range(2):
                copies.append(
                    pltpu.make_async_copy(
                        total_ref.at[r // chunk, j].reshape(fields, chunk, lanes),
                        out_hbm.at[:, pl.ds(r + 1 - chunk, chunk), pl.ds(j * lanes, lanes)],
                        sems.at[r // chunk, j],
                    )
                )
                copies[-1].start()
    for copy in copies:
        copy.wait()


def merge_kernel(level, count, first, *refs):
    refs = list(refs)
    own_ref, other_ref, coeffs_ref = refs[:3]
    sums_ref = None if first else refs[3]
    held_ref, sum_ref = refs[-2:] if not first else refs[5:7]
    place = lax.axis_index("rad")
    upper = iota((own_ref.shape[-2], LANES), 0) * 0 + (place & (1 << level)) != 0
    following = iota((own_ref.shape[-2], LANES), 0) * 0 + (place & (2 << level)) != 0
    q, own, other_scale, felt_l, felt_r, b, c = [coeffs_ref[7 * level + i] for i in range(7)]
    for t in range(own_ref.shape[1]):
        head, tail = own_ref[0, t], own_ref[1, t]
        meeting = jnp.where(upper, other_ref[1, t], other_ref[0, t])
        facing = jnp.where(upper, head, tail)
        inner = q * meeting + own * facing
        partner = q * facing + other_scale * meeting
        if first:
            sum_ref[0, t] = felt_l * inner
            sum_ref[1, t] = felt_r * inner
        else:
            sum_ref[0, t] = sums_ref[0, t] + felt_l * inner
            sum_ref[1, t] = sums_ref[1, t] + felt_r * inner
        head = jnp.where(upper, other_ref[0, t], head) + c * jnp.where(upper, partner, inner)
        tail = jnp.where(upper, tail, other_ref[1, t]) + b * jnp.where(upper, inner, partner)
        if 4 << level == count:
            held_ref[t] = jnp.where(following, head, tail)
        else:
            held_ref[0, t] = head
            held_ref[1, t] = tail


def merge(level, held, coeffs, extra):
    count = lax.axis_size("rad")
    first = level == 0
    last = 4 << level == count
    sums = pltpu.VMEM(held.shape, f32)
    message = pltpu.VMEM(held.shape[1:] if last else held.shape, f32)
    return pl.pallas_call(
        functools.partial(merge_kernel, level, count, first),
        out_shape=[pltpu.VMEM(extra.shape, f32), message, sums] if first else [message, sums],
        in_specs=[VMEM] * 4,
        out_specs=[VMEM] * (3 if first else 2),
        input_output_aliases={3: 0} if first else {},
        cost_estimate=cost(40000),
        name="merge",
    )(*map(in_vmem, (held, swapped(held, "rad", 1 << level), coeffs, extra)))


def join_kernel(own_ref, other_ref, coeffs_ref, sums_ref, out_ref):
    for e in range(2):
        for t in range(own_ref.shape[0]):
            out_ref[0, e, t] = (
                sums_ref[e, t]
                + coeffs_ref[2 * e] * other_ref[t]
                + coeffs_ref[2 * e + 1] * own_ref[t]
            )


def per_device(state, velocity, coupling, diffusivity, inverse, shifts):
    state = state[:, 0]
    fields, rows, cells = state.shape
    tiles = cells // LANES
    assert tiles == 2 and fields == 8 and 2 * rows <= LANES
    count = lax.axis_size("az")
    segments = lax.axis_size("rad")
    offsets, state_near, inverse_near = pl.pallas_call(
        offsets_kernel,
        out_shape=[
            pltpu.VMEM((2, tiles + 1, fields, LANES), f32),
            pltpu.VMEM(state.shape, f32),
            pltpu.VMEM(inverse.shape, f32),
        ],
        in_specs=[ANY] * 5,
        out_specs=[VMEM] * 3,
        scratch_shapes=[
            pltpu.VMEM((1, rows), f32),
            pltpu.VMEM((fields, fields), f32),
            pltpu.VMEM((1, fields), f32),
            pltpu.SemaphoreType.DMA((5,)),
        ],
        cost_estimate=cost(5000),
        name="offsets",
    )(state, inverse, velocity[None], coupling, diffusivity[None])
    spare = count * 2 * rows // cells
    solved, columns, coeffs, final = pl.pallas_call(
        functools.partial(solve_kernel, count, segments),
        out_shape=[
            pltpu.VMEM((rows + spare, tiles, fields, LANES), f32),
            pltpu.VMEM((2, rows, fields, LANES), f32),
            pltpu.VMEM((7 * log2(segments) - 7, fields, LANES), f32),
            pltpu.VMEM((4, fields, LANES), f32),
        ],
        in_specs=[SMEM] + [VMEM] * 4,
        out_specs=[VMEM] * 4,
        scratch_shapes=[
            pltpu.VMEM((fields, rows, cells), f32),
            pltpu.VMEM((fields * rows, cells + LANES), f32),
            pltpu.VMEM((fields * rows // LANES, fields * rows, LANES), f32),
        ],
        cost_estimate=cost(8000),
        name="solve",
    )(coupling, in_vmem(state_near), velocity[None], diffusivity[None], in_vmem(inverse_near))
    kept, held, sums = merge(0, offsets, coeffs, solved)
    bit = 1
    while 2 * bit < count:
        kept, coeffs = pl.pallas_call(
            functools.partial(select_kernel, bit),
            out_shape=[pltpu.VMEM(kept.shape, f32), pltpu.VMEM(coeffs.shape, f32)],
            in_specs=[SMEM] + [VMEM] * 3,
            out_specs=[VMEM] * 2,
            cost_estimate=cost(2800),
        name="select",
        )(shifts, in_vmem(kept), in_vmem(swapped(kept, "az", bit)), in_vmem(coeffs))
        bit *= 2
    rotated = pl.pallas_call(
        functools.partial(rotate_kernel, count, bit),
        out_shape=pltpu.VMEM((rows, tiles, fields, LANES), f32),
        in_specs=[SMEM] + [VMEM] * 2,
        out_specs=VMEM,
        scratch_shapes=[pltpu.VMEM((count * 2 * rows // LANES, fields, LANES), f32)],
        cost_estimate=cost(4000),
        name="rotate",
    )(shifts, in_vmem(kept), in_vmem(swapped(kept, "az", bit)))
    for level in range(1, log2(segments) - 1):
        held, sums = merge(level, held, coeffs, sums)
    forcing = pl.pallas_call(
        join_kernel,
        out_shape=pltpu.VMEM((1,) + sums.shape, f32),
        in_specs=[VMEM] * 4,
        out_specs=VMEM,
        cost_estimate=cost(400),
        name="join",
    )(*map(in_vmem, (held, swapped(held, "rad", segments // 2), final, sums)))
    parts = [forcing]
    bit = 1
    while bit < count:
        parts.append(swapped(jnp.concatenate(parts, 0), "az", bit))
        bit *= 2
    out = pl.pallas_call(
        functools.partial(finish_kernel, count, len(parts)),
        out_shape=jax.ShapeDtypeStruct(state.shape, f32),
        in_specs=[SMEM] + [VMEM] * (2 + len(parts)),
        out_specs=ANY,
        scratch_shapes=[
            pltpu.VMEM((count, 2, tiles + 1, fields, LANES), f32),
            pltpu.VMEM((rows // 8, tiles, 8 * fields, LANES), f32),
            pltpu.SemaphoreType.DMA((rows // 8, tiles)),
        ],
        cost_estimate=cost(6000),
        name="finish",
    )(shifts, in_vmem(columns), in_vmem(rotated), *map(in_vmem, parts))
    return out[:, None]


def solution(mesh):
    return jax.shard_map(
        per_device,
        mesh=mesh,
        in_specs=(P(None, None, "rad", "az"), P("rad"), P(), P(), P(), P("rad")),
        out_specs=P(None, None, "rad", "az"),
        check_vma=False,
    )
```

```python
import functools

import jax
import jax.numpy as jnp
from jax import lax
from jax.experimental import pallas as pl
from jax.experimental.pallas import tpu as pltpu
from jax.sharding import PartitionSpec as P

highest = lax.Precision.HIGHEST
f32 = jnp.float32
LANES = 128
BATCH = 8
SMEM = pl.BlockSpec(memory_space=pltpu.SMEM)
VMEM = pl.BlockSpec(memory_space=pltpu.VMEM)
ANY = pl.BlockSpec(memory_space=pl.ANY)


def cost(kilobytes):
    return pl.CostEstimate(flops=kilobytes << 18, bytes_accessed=kilobytes << 10, transcendentals=0)


def in_vmem(x):
    return pltpu.with_memory_space_constraint(x, pltpu.VMEM)


def in_smem(x):
    return pltpu.with_memory_space_constraint(x, pltpu.SMEM)


def iota(shape, dim):
    return lax.broadcasted_iota(jnp.int32, shape, dim)


def log2(number):
    assert number & (number - 1) == 0
    return number.bit_length() - 1


def swapped(block, axis, bit):
    return lax.ppermute(block, axis, [(i, i ^ bit) for i in range(lax.axis_size(axis))])


def tile(x, j):
    return x[:, j * LANES : (j + 1) * LANES]


def as_column(row):
    n = row.shape[1]
    same = iota((n, n), 0) == iota((n, n), 1)
    return jnp.sum(jnp.where(same, jnp.broadcast_to(row, (n, n)), 0.0), axis=1, keepdims=True)


def level_coefficients(first, last, count, place):
    fields = first.shape[0]
    wide = (fields, LANES)
    a = jnp.broadcast_to(first[:, :1], wide)
    b = jnp.broadcast_to(last[:, :1], wide)
    c = jnp.broadcast_to(first[:, -1:], wide)
    d = jnp.broadcast_to(last[:, -1:], wide)
    one, none = jnp.ones(wide, f32), jnp.zeros(wide, f32)
    left_l, left_r, right_l, right_r = one, none, none, one
    found = []
    bit = 1
    while bit < count:
        side = iota(wide, 0) * 0 + (place & bit)
        upper = side != 0
        q = 1.0 / (1.0 - a * d)
        own = q * jnp.where(upper, d, a)
        felt_l = jnp.where(upper, left_l, left_r)
        felt_r = jnp.where(upper, right_l, right_r)
        if 2 * bit == count:
            found += [felt_l * q, felt_l * own, felt_r * q, felt_r * own]
            break
        found += [q, own, q * jnp.where(upper, a, d), felt_l, felt_r, b, c]
        via_l = jnp.where(upper, b * q, a * b * q)
        via_r = jnp.where(upper, c * d * q, c * q)
        left_l, left_r = (
            jnp.where(upper, none, left_l) + felt_l * via_l,
            jnp.where(upper, left_r, none) + felt_l * via_r,
        )
        right_l, right_r = (
            jnp.where(upper, none, right_l) + felt_r * via_l,
            jnp.where(upper, right_r, none) + felt_r * via_r,
        )
        a, b, c, d = a + a * b * c * q, b * b * q, c * c * q, d + b * c * d * q
        bit *= 2
    return found


def offsets_kernel(
    state_hbm, inverse_hbm, velocity_hbm, coupling_hbm, diffusivity_hbm, shifts_hbm,
    out_ref, state_ref, inverse_ref, velocity_ref, diffusivity_ref, shifts_ref, mixing_ref,
    coupling_ref, sems,
):
    copies = [
        pltpu.make_async_copy(source, target, sems.at[i])
        for i, (source, target) in enumerate(
            (
                (inverse_hbm, inverse_ref),
                (velocity_hbm, velocity_ref),
                (coupling_hbm, coupling_ref),
                (diffusivity_hbm, diffusivity_ref),
                (state_hbm, state_ref),
                (shifts_hbm, shifts_ref),
                (coupling_hbm, mixing_ref),
            )
        )
    ]
    for copy in copies:
        copy.start()
    for copy in copies[:4]:
        copy.wait()
    fields, rows, cells = state_ref.shape
    span = fields * rows
    diffusivity = as_column(diffusivity_ref[...])
    first = diffusivity * inverse_ref[:, 0, :]
    last = diffusivity * inverse_ref[:, rows - 1, :]
    first = jnp.concatenate([first] * fields, axis=1)
    last = jnp.concatenate([last] * fields, axis=1)
    speed = jnp.concatenate([jnp.broadcast_to(velocity_ref[...], (fields, rows))] * fields, axis=1)
    lane = iota((fields, span), 1)
    row = lane & (rows - 1)
    group = lane >> log2(rows)
    own = group == iota((fields, span), 0)
    mix = jnp.zeros((fields, span), f32)
    for g in range(fields):
        mix = jnp.where(group == g, coupling_ref[:, g : g + 1], mix)
    weights = []
    drift = []
    for vector, below, above in ((first, 1.0, 0.0), (last, 0.0, 1.0)):
        lower = jnp.where(row == 0, below, pltpu.roll(vector, 1, 1))
        upper = jnp.where(row == rows - 1, above, pltpu.roll(vector, span - 1, 1))
        weights.append(jnp.where(own, vector, 0.0) + 0.5 * mix * (lower - upper))
        drift.append(jnp.where(own, 0.5 * speed * vector, 0.0))
    table = jnp.concatenate(weights + drift, axis=0)
    copies[4].wait()
    sums = jnp.dot(
        table,
        state_ref[...].reshape(span, cells),
        precision=highest,
        preferred_element_type=f32,
    )
    blank = jnp.zeros((2 * fields, LANES), f32)
    main = jnp.concatenate([sums[: 2 * fields], blank], axis=1)
    side = jnp.concatenate([sums[2 * fields :], blank], axis=1)
    width = cells + LANES
    total = main + pltpu.roll(side, 1, 1) - pltpu.roll(side, width - 1, 1)
    for e in range(2):
        for j in range(width // LANES):
            out_ref[e, j] = tile(total[e * fields : (e + 1) * fields], j)
    for copy in copies[5:]:
        copy.wait()


def solve_kernel(
    count, segments, coupling_ref, state_ref, velocity_ref, diffusivity_ref, inverse_ref,
    out_ref, columns_ref, coeffs_ref, final_ref, diff_ref, updated_ref, table_ref,
):
    fields, rows, cells = state_ref.shape
    span = fields * rows
    width = cells + LANES
    row = iota((rows, cells), 0)
    half = 0.5 * as_column(velocity_ref[...])
    diffusivity = as_column(diffusivity_ref[...])
    first = diffusivity * inverse_ref[:, 0, :]
    last = diffusivity * inverse_ref[:, rows - 1, :]
    for i, x in enumerate(level_coefficients(first, last, segments, lax.axis_index("rad"))):
        if i < coeffs_ref.shape[0]:
            coeffs_ref[i] = x
        else:
            final_ref[i - coeffs_ref.shape[0]] = x
    for g in range(fields):
        block = state_ref[g]
        upper = jnp.where(row == rows - 1, 0.0, pltpu.roll(block, rows - 1, 0))
        lower = jnp.where(row == 0, 0.0, pltpu.roll(block, 1, 0))
        diff_ref[g] = 0.5 * (upper - lower)
        padded = jnp.concatenate([block, jnp.zeros((rows, LANES), f32)], axis=1)
        updated_ref[g * rows : (g + 1) * rows] = padded + half * (
            pltpu.roll(padded, 1, 1) - pltpu.roll(padded, width - 1, 1)
        )
        pad = [jnp.zeros((rows, rows), f32)] * fields
        pad[g] = inverse_ref[g]
        placed = jnp.concatenate(pad, axis=1)
        for j in range(span // LANES):
            table_ref[j, pl.ds(g, rows, stride=fields), :] = tile(placed, j)
    for f in range(fields):
        total = updated_ref[f * rows : (f + 1) * rows, :cells]
        for g in range(fields):
            total = total + coupling_ref[f, g] * diff_ref[g]
        updated_ref[f * rows : (f + 1) * rows, :cells] = total
    solved = jnp.dot(
        jnp.concatenate([table_ref[j] for j in range(span // LANES)], axis=1),
        updated_ref[...],
        precision=highest,
        preferred_element_type=f32,
    )
    lane = iota((fields, LANES), 1)
    ghosts = jnp.zeros((fields, LANES), f32)
    for r in range(rows):
        block = solved[r * fields : (r + 1) * fields]
        out_ref[r, 0] = tile(block, 0)
        out_ref[r, 1] = tile(block, 1)
        edge = tile(block, 2)
        ghosts = jnp.where(lane == r, pltpu.roll(edge, r, 1), ghosts)
        ghosts = jnp.where(lane == rows + r, pltpu.roll(edge, rows + r + 1, 1), ghosts)
        columns_ref[0, r] = jnp.broadcast_to(inverse_ref[:, r, :1], (fields, LANES))
        columns_ref[1, r] = jnp.broadcast_to(inverse_ref[:, r, rows - 1 :], (fields, LANES))
    place = lax.axis_index("az")
    for at in range(count * 2 * rows // LANES):
        for part in range(LANES // (2 * rows)):
            mine = iota((fields, LANES), 0) * 0 + place == at * (LANES // (2 * rows)) + part
            moved = pltpu.roll(ghosts, part * 2 * rows, 1) if part else ghosts
            value = jnp.where(mine, moved, 0.0)
            total = value if part == 0 else total + value
        out_ref[rows + at // 2, at % 2] = total


def masks(shift, cells, place, bit):
    residue = shift & (cells - 1)
    hops = shift >> log2(cells)
    near = ((place - hops) ^ place) & bit
    far = ((place - hops - 1) ^ place) & bit
    lane = iota((8, LANES), 1)
    return [jnp.where(lane + j * LANES < cells - residue, near, far) != 0 for j in range(2)]


def select_kernel(bit, shifts_ref, kept_ref, came_ref, coeffs_ref, out_ref, later_ref):
    later_ref[...] = coeffs_ref[...]
    rows = shifts_ref.shape[0]
    place = lax.axis_index("az")
    for batch in range(0, rows, BATCH):
        values = []
        for r in range(batch, batch + BATCH):
            take = masks(shifts_ref[r], 2 * LANES, place, bit)
            values.append([jnp.where(take[j], came_ref[r, j], kept_ref[r, j]) for j in range(2)])
        for r, value in zip(range(batch, batch + BATCH), values):
            for j in range(2):
                out_ref[r, j] = value[j]
    out_ref[rows:] = kept_ref[rows:] + came_ref[rows:]


def turned(value, residue):
    amount = residue & (LANES - 1)
    low = iota(value[0].shape, 1) < amount
    turn = [pltpu.roll(x, amount, 1) for x in value]
    return [jnp.where(low, turn[1], turn[0]), jnp.where(low, turn[0], turn[1])]


def rotate_kernel(count, bit, shifts_ref, kept_ref, came_ref, out_ref, ghosts_ref):
    rows, tiles, fields, lanes = out_ref.shape
    cells = tiles * lanes
    per_tile = lanes // (2 * rows)
    place = lax.axis_index("az")
    lane = iota((fields, lanes), 1)
    for at in range(count * 2 * rows // lanes):
        ghosts_ref[at] = kept_ref[rows + at // 2, at % 2] + came_ref[rows + at // 2, at % 2]
    for batch in range(0, rows, BATCH):
        values = []
        for r in range(batch, batch + BATCH):
            shift = shifts_ref[r]
            hops = shift >> log2(cells)
            residue = shift & (cells - 1)
            take = masks(shift, cells, place, bit)
            value = [jnp.where(take[j], came_ref[r, j], kept_ref[r, j]) for j in range(2)]
            here = (place - hops) & (count - 1)
            before = (here - 1) & (count - 1)
            after = jnp.where(residue > 0, here, (here + 1) & (count - 1))
            low_at = (before & (per_tile - 1)) * 2 * rows + r
            high_at = (after & (per_tile - 1)) * 2 * rows + rows + r
            low = pltpu.roll(ghosts_ref[before >> log2(per_tile)], (lanes - low_at) & (lanes - 1), 1)
            high = pltpu.roll(ghosts_ref[after >> log2(per_tile)], lanes - 1 - high_at, 1)
            value[0] = value[0] + jnp.where(lane == 0, low, 0.0)
            value[1] = value[1] + jnp.where(lane == lanes - 1, high, 0.0)
            values.append((r, residue >> log2(lanes), turned(value, residue)))
        for r, swap, value in values:
            out_ref[r, swap] = value[0]
            out_ref[r, 1 - swap] = value[1]


def finish_kernel(count, parts, shifts_ref, columns_ref, rotated_ref, *rest):
    out_hbm, forcing_ref, total_ref, sems = rest[parts:]
    rows, tiles, fields, lanes = rotated_ref.shape
    cells = tiles * lanes
    at = 0
    place = lax.axis_index("az")
    lane = iota((fields, lanes), 1)
    for part in rest[:parts]:
        forcing_ref[at : at + part.shape[0]] = part[...]
        at += part.shape[0]
    for m in range(count):
        before = (((place ^ m) - 1) & (count - 1)) ^ place
        after = (((place ^ m) + 1) & (count - 1)) ^ place
        for e in range(2):
            forcing_ref[m, e, 0] += jnp.where(lane == 0, forcing_ref[before, e, tiles], 0.0)
            forcing_ref[m, e, 1] += jnp.where(lane == lanes - 1, forcing_ref[after, e, tiles], 0.0)
    copies = []
    for batch in range(0, rows, BATCH):
        values = []
        for r in range(batch, batch + BATCH):
            shift = shifts_ref[r]
            hops = shift >> log2(cells)
            residue = shift & (cells - 1)
            here = (place - hops) & (count - 1)
            source = here ^ place
            source_low = ((here - 1) & (count - 1)) ^ place
            value = []
            for j in range(2):
                near = lane + j * lanes < cells - residue
                left = jnp.where(near, forcing_ref[source, 0, j], forcing_ref[source_low, 0, j])
                right = jnp.where(near, forcing_ref[source, 1, j], forcing_ref[source_low, 1, j])
                value.append(columns_ref[0, r] * left + columns_ref[1, r] * right)
            value = turned(value, residue)
            swap = residue >> log2(lanes)
            values.append(
                (swap, value[0] + rotated_ref[r, swap], value[1] + rotated_ref[r, 1 - swap])
            )
        at = batch // BATCH
        for i, (swap, near, far) in enumerate(values):
            total_ref[at, swap, pl.ds(i, fields, stride=BATCH), :] = near
            total_ref[at, 1 - swap, pl.ds(i, fields, stride=BATCH), :] = far
        for j in range(2):
            copies.append(
                pltpu.make_async_copy(
                    total_ref.at[at, j].reshape(fields, BATCH, lanes),
                    out_hbm.at[:, pl.ds(batch, BATCH), pl.ds(j * lanes, lanes)],
                    sems.at[at, j],
                )
            )
            copies[-1].start()
    for copy in copies:
        copy.wait()


def merge_kernel(level, count, first, *refs):
    refs = list(refs)
    own_ref, other_ref, coeffs_ref = refs[:3]
    sums_ref = None if first else refs[3]
    held_ref, sum_ref = refs[-2:] if not first else refs[5:7]
    place = lax.axis_index("rad")
    upper = iota((own_ref.shape[-2], LANES), 0) * 0 + (place & (1 << level)) != 0
    following = iota((own_ref.shape[-2], LANES), 0) * 0 + (place & (2 << level)) != 0
    q, own, other_scale, felt_l, felt_r, b, c = [coeffs_ref[7 * level + i] for i in range(7)]
    for t in range(own_ref.shape[1]):
        head, tail = own_ref[0, t], own_ref[1, t]
        meeting = jnp.where(upper, other_ref[1, t], other_ref[0, t])
        facing = jnp.where(upper, head, tail)
        inner = q * meeting + own * facing
        partner = q * facing + other_scale * meeting
        if first:
            sum_ref[0, t] = felt_l * inner
            sum_ref[1, t] = felt_r * inner
        else:
            sum_ref[0, t] = sums_ref[0, t] + felt_l * inner
            sum_ref[1, t] = sums_ref[1, t] + felt_r * inner
        head = jnp.where(upper, other_ref[0, t], head) + c * jnp.where(upper, partner, inner)
        tail = jnp.where(upper, tail, other_ref[1, t]) + b * jnp.where(upper, inner, partner)
        if 4 << level == count:
            held_ref[t] = jnp.where(following, head, tail)
        else:
            held_ref[0, t] = head
            held_ref[1, t] = tail


def merge(level, held, coeffs, extra):
    count = lax.axis_size("rad")
    first = level == 0
    last = 4 << level == count
    sums = pltpu.VMEM(held.shape, f32)
    message = pltpu.VMEM(held.shape[1:] if last else held.shape, f32)
    return pl.pallas_call(
        functools.partial(merge_kernel, level, count, first),
        out_shape=[pltpu.VMEM(extra.shape, f32), message, sums] if first else [message, sums],
        in_specs=[VMEM] * 4,
        out_specs=[VMEM] * (3 if first else 2),
        input_output_aliases={3: 0} if first else {},
        cost_estimate=cost(40000),
        name="merge",
    )(*map(in_vmem, (held, swapped(held, "rad", 1 << level), coeffs, extra)))


def join_kernel(own_ref, other_ref, coeffs_ref, sums_ref, out_ref):
    for e in range(2):
        for t in range(own_ref.shape[0]):
            out_ref[0, e, t] = (
                sums_ref[e, t]
                + coeffs_ref[2 * e] * other_ref[t]
                + coeffs_ref[2 * e + 1] * own_ref[t]
            )


def per_device(state, velocity, coupling, diffusivity, inverse, shifts):
    state = state[:, 0]
    fields, rows, cells = state.shape
    tiles = cells // LANES
    assert tiles == 2 and fields == 8 and 2 * rows <= LANES
    count = lax.axis_size("az")
    segments = lax.axis_size("rad")
    offsets, state_near, inverse_near, velocity, diffusivity, shifts, mixing = pl.pallas_call(
        offsets_kernel,
        out_shape=[
            pltpu.VMEM((2, tiles + 1, fields, LANES), f32),
            pltpu.VMEM(state.shape, f32),
            pltpu.VMEM(inverse.shape, f32),
            pltpu.VMEM((1, rows), f32),
            pltpu.VMEM((1, fields), f32),
            pltpu.SMEM(shifts.shape, jnp.int32),
            pltpu.SMEM(coupling.shape, f32),
        ],
        in_specs=[ANY] * 6,
        out_specs=[VMEM] * 5 + [SMEM] * 2,
        scratch_shapes=[
            pltpu.VMEM((fields, fields), f32),
            pltpu.SemaphoreType.DMA((7,)),
        ],
        cost_estimate=cost(5000),
        name="offsets",
    )(state, inverse, velocity[None], coupling, diffusivity[None], shifts)
    shifts = in_smem(shifts)
    spare = count * 2 * rows // cells
    solved, columns, coeffs, final = pl.pallas_call(
        functools.partial(solve_kernel, count, segments),
        out_shape=[
            pltpu.VMEM((rows + spare, tiles, fields, LANES), f32),
            pltpu.VMEM((2, rows, fields, LANES), f32),
            pltpu.VMEM((7 * log2(segments) - 7, fields, LANES), f32),
            pltpu.VMEM((4, fields, LANES), f32),
        ],
        in_specs=[SMEM] + [VMEM] * 4,
        out_specs=[VMEM] * 4,
        scratch_shapes=[
            pltpu.VMEM((fields, rows, cells), f32),
            pltpu.VMEM((fields * rows, cells + LANES), f32),
            pltpu.VMEM((fields * rows // LANES, fields * rows, LANES), f32),
        ],
        cost_estimate=cost(8000),
        name="solve",
    )(in_smem(mixing), *map(in_vmem, (state_near, velocity, diffusivity, inverse_near)))
    kept, held, sums = merge(0, offsets, coeffs, solved)
    bit = 1
    while 2 * bit < count:
        kept, coeffs = pl.pallas_call(
            functools.partial(select_kernel, bit),
            out_shape=[pltpu.VMEM(kept.shape, f32), pltpu.VMEM(coeffs.shape, f32)],
            in_specs=[SMEM] + [VMEM] * 3,
            out_specs=[VMEM] * 2,
            cost_estimate=cost(2800),
        name="select",
        )(shifts, in_vmem(kept), in_vmem(swapped(kept, "az", bit)), in_vmem(coeffs))
        bit *= 2
    rotated = pl.pallas_call(
        functools.partial(rotate_kernel, count, bit),
        out_shape=pltpu.VMEM((rows, tiles, fields, LANES), f32),
        in_specs=[SMEM] + [VMEM] * 2,
        out_specs=VMEM,
        scratch_shapes=[pltpu.VMEM((count * 2 * rows // LANES, fields, LANES), f32)],
        cost_estimate=cost(4000),
        name="rotate",
    )(shifts, in_vmem(kept), in_vmem(swapped(kept, "az", bit)))
    for level in range(1, log2(segments) - 1):
        held, sums = merge(level, held, coeffs, sums)
    forcing = pl.pallas_call(
        join_kernel,
        out_shape=pltpu.VMEM((1,) + sums.shape, f32),
        in_specs=[VMEM] * 4,
        out_specs=VMEM,
        cost_estimate=cost(400),
        name="join",
    )(*map(in_vmem, (held, swapped(held, "rad", segments // 2), final, sums)))
    parts = [forcing]
    bit = 1
    while bit < count:
        ours = parts[0] if len(parts) == 1 else jnp.concatenate(parts, 0)
        parts += [swapped(ours, "az", i * bit) for i in range(1, min(4, count // bit))]
        bit *= 4
    out = pl.pallas_call(
        functools.partial(finish_kernel, count, len(parts)),
        out_shape=jax.ShapeDtypeStruct(state.shape, f32),
        in_specs=[SMEM] + [VMEM] * (2 + len(parts)),
        out_specs=ANY,
        scratch_shapes=[
            pltpu.VMEM((count, 2, tiles + 1, fields, LANES), f32),
            pltpu.VMEM((rows // BATCH, tiles, BATCH * fields, LANES), f32),
            pltpu.SemaphoreType.DMA((rows // BATCH, tiles)),
        ],
        cost_estimate=cost(6000),
        name="finish",
    )(shifts, in_vmem(columns), in_vmem(rotated), *map(in_vmem, parts))
    return out[:, None]


def solution(mesh):
    return jax.shard_map(
        per_device,
        mesh=mesh,
        in_specs=(P(None, None, "rad", "az"), P("rad"), P(), P(), P(), P("rad")),
        out_specs=P(None, None, "rad", "az"),
        check_vma=False,
    )
```

```python
import functools

import jax
import jax.numpy as jnp
from jax import lax
from jax.experimental import pallas as pl
from jax.experimental.pallas import tpu as pltpu
from jax.sharding import PartitionSpec as P

highest = lax.Precision.HIGHEST
f32 = jnp.float32
LANES = 128
BATCH = 8
SMEM = pl.BlockSpec(memory_space=pltpu.SMEM)
VMEM = pl.BlockSpec(memory_space=pltpu.VMEM)
ANY = pl.BlockSpec(memory_space=pl.ANY)


def cost(kilobytes):
    return pl.CostEstimate(flops=kilobytes << 18, bytes_accessed=kilobytes << 10, transcendentals=0)


def in_vmem(x):
    return pltpu.with_memory_space_constraint(x, pltpu.VMEM)


def in_smem(x):
    return pltpu.with_memory_space_constraint(x, pltpu.SMEM)


def iota(shape, dim):
    return lax.broadcasted_iota(jnp.int32, shape, dim)


def log2(number):
    assert number & (number - 1) == 0
    return number.bit_length() - 1


def swapped(block, axis, bit):
    return lax.ppermute(block, axis, [(i, i ^ bit) for i in range(lax.axis_size(axis))])


def tile(x, j):
    return x[:, j * LANES : (j + 1) * LANES]


def as_column(row):
    n = row.shape[1]
    same = iota((n, n), 0) == iota((n, n), 1)
    return jnp.sum(jnp.where(same, jnp.broadcast_to(row, (n, n)), 0.0), axis=1, keepdims=True)


def level_coefficients(first, last, count, place):
    fields = first.shape[0]
    wide = (fields, LANES)
    a = jnp.broadcast_to(first[:, :1], wide)
    b = jnp.broadcast_to(last[:, :1], wide)
    c = jnp.broadcast_to(first[:, -1:], wide)
    d = jnp.broadcast_to(last[:, -1:], wide)
    one, none = jnp.ones(wide, f32), jnp.zeros(wide, f32)
    left_l, left_r, right_l, right_r = one, none, none, one
    found = []
    bit = 1
    while bit < count:
        side = iota(wide, 0) * 0 + (place & bit)
        upper = side != 0
        q = 1.0 / (1.0 - a * d)
        own = q * jnp.where(upper, d, a)
        felt_l = jnp.where(upper, left_l, left_r)
        felt_r = jnp.where(upper, right_l, right_r)
        if 2 * bit == count:
            found += [felt_l * q, felt_l * own, felt_r * q, felt_r * own]
            break
        found += [q, own, q * jnp.where(upper, a, d), felt_l, felt_r, b, c]
        via_l = jnp.where(upper, b * q, a * b * q)
        via_r = jnp.where(upper, c * d * q, c * q)
        left_l, left_r = (
            jnp.where(upper, none, left_l) + felt_l * via_l,
            jnp.where(upper, left_r, none) + felt_l * via_r,
        )
        right_l, right_r = (
            jnp.where(upper, none, right_l) + felt_r * via_l,
            jnp.where(upper, right_r, none) + felt_r * via_r,
        )
        a, b, c, d = a + a * b * c * q, b * b * q, c * c * q, d + b * c * d * q
        bit *= 2
    return found


def offsets_kernel(
    state_hbm, inverse_hbm, velocity_hbm, coupling_hbm, diffusivity_hbm, shifts_hbm,
    out_ref, state_ref, velocity_ref, diffusivity_ref, shifts_ref, mixing_ref,
    first_ref, last_ref, coupling_ref, sems,
):
    fields, rows, cells = state_ref.shape
    copies = [
        pltpu.make_async_copy(source, target, sems.at[i])
        for i, (source, target) in enumerate(
            (
                (inverse_hbm.at[:, :8], first_ref),
                (inverse_hbm.at[:, rows - 8 :], last_ref),
                (coupling_hbm, coupling_ref),
                (velocity_hbm, velocity_ref),
                (diffusivity_hbm, diffusivity_ref),
                (state_hbm, state_ref),
                (shifts_hbm, shifts_ref),
                (coupling_hbm, mixing_ref),
            )
        )
    ]
    for copy in copies:
        copy.start()
    for copy in copies[:5]:
        copy.wait()
    span = fields * rows
    diffusivity = as_column(diffusivity_ref[...])
    first = diffusivity * first_ref[:, 0, :]
    last = diffusivity * last_ref[:, 7, :]
    first = jnp.concatenate([first] * fields, axis=1)
    last = jnp.concatenate([last] * fields, axis=1)
    speed = jnp.concatenate([jnp.broadcast_to(velocity_ref[...], (fields, rows))] * fields, axis=1)
    lane = iota((fields, span), 1)
    row = lane & (rows - 1)
    group = lane >> log2(rows)
    own = group == iota((fields, span), 0)
    mix = jnp.zeros((fields, span), f32)
    for g in range(fields):
        mix = jnp.where(group == g, coupling_ref[:, g : g + 1], mix)
    weights = []
    drift = []
    for vector, below, above in ((first, 1.0, 0.0), (last, 0.0, 1.0)):
        lower = jnp.where(row == 0, below, pltpu.roll(vector, 1, 1))
        upper = jnp.where(row == rows - 1, above, pltpu.roll(vector, span - 1, 1))
        weights.append(jnp.where(own, vector, 0.0) + 0.5 * mix * (lower - upper))
        drift.append(jnp.where(own, 0.5 * speed * vector, 0.0))
    table = jnp.concatenate(weights + drift, axis=0)
    copies[5].wait()
    sums = jnp.dot(
        table,
        state_ref[...].reshape(span, cells),
        precision=highest,
        preferred_element_type=f32,
    )
    blank = jnp.zeros((2 * fields, LANES), f32)
    main = jnp.concatenate([sums[: 2 * fields], blank], axis=1)
    side = jnp.concatenate([sums[2 * fields :], blank], axis=1)
    width = cells + LANES
    total = main + pltpu.roll(side, 1, 1) - pltpu.roll(side, width - 1, 1)
    for e in range(2):
        for j in range(width // LANES):
            out_ref[e, j] = tile(total[e * fields : (e + 1) * fields], j)
    for copy in copies[6:]:
        copy.wait()


def solve_kernel(
    count, segments, coupling_ref, state_ref, velocity_ref, diffusivity_ref, inverse_ref,
    out_ref, columns_ref, coeffs_ref, final_ref, diff_ref, updated_ref, table_ref,
):
    fields, rows, cells = state_ref.shape
    span = fields * rows
    width = cells + LANES
    row = iota((rows, cells), 0)
    half = 0.5 * as_column(velocity_ref[...])
    diffusivity = as_column(diffusivity_ref[...])
    first = diffusivity * inverse_ref[:, 0, :]
    last = diffusivity * inverse_ref[:, rows - 1, :]
    for i, x in enumerate(level_coefficients(first, last, segments, lax.axis_index("rad"))):
        if i < coeffs_ref.shape[0]:
            coeffs_ref[i] = x
        else:
            final_ref[i - coeffs_ref.shape[0]] = x
    for g in range(fields):
        block = state_ref[g]
        upper = jnp.where(row == rows - 1, 0.0, pltpu.roll(block, rows - 1, 0))
        lower = jnp.where(row == 0, 0.0, pltpu.roll(block, 1, 0))
        diff_ref[g] = 0.5 * (upper - lower)
        padded = jnp.concatenate([block, jnp.zeros((rows, LANES), f32)], axis=1)
        updated_ref[g * rows : (g + 1) * rows] = padded + half * (
            pltpu.roll(padded, 1, 1) - pltpu.roll(padded, width - 1, 1)
        )
        pad = [jnp.zeros((rows, rows), f32)] * fields
        pad[g] = inverse_ref[g]
        placed = jnp.concatenate(pad, axis=1)
        for j in range(span // LANES):
            table_ref[j, pl.ds(g, rows, stride=fields), :] = tile(placed, j)
    for f in range(fields):
        total = updated_ref[f * rows : (f + 1) * rows, :cells]
        for g in range(fields):
            total = total + coupling_ref[f, g] * diff_ref[g]
        updated_ref[f * rows : (f + 1) * rows, :cells] = total
    solved = jnp.dot(
        jnp.concatenate([table_ref[j] for j in range(span // LANES)], axis=1),
        updated_ref[...],
        precision=highest,
        preferred_element_type=f32,
    )
    lane = iota((fields, LANES), 1)
    ghosts = jnp.zeros((fields, LANES), f32)
    for r in range(rows):
        block = solved[r * fields : (r + 1) * fields]
        out_ref[r, 0] = tile(block, 0)
        out_ref[r, 1] = tile(block, 1)
        edge = tile(block, 2)
        ghosts = jnp.where(lane == r, pltpu.roll(edge, r, 1), ghosts)
        ghosts = jnp.where(lane == rows + r, pltpu.roll(edge, rows + r + 1, 1), ghosts)
        columns_ref[0, r] = jnp.broadcast_to(inverse_ref[:, r, :1], (fields, LANES))
        columns_ref[1, r] = jnp.broadcast_to(inverse_ref[:, r, rows - 1 :], (fields, LANES))
    place = lax.axis_index("az")
    for at in range(count * 2 * rows // LANES):
        for part in range(LANES // (2 * rows)):
            mine = iota((fields, LANES), 0) * 0 + place == at * (LANES // (2 * rows)) + part
            moved = pltpu.roll(ghosts, part * 2 * rows, 1) if part else ghosts
            value = jnp.where(mine, moved, 0.0)
            total = value if part == 0 else total + value
        out_ref[rows + at // 2, at % 2] = total


def masks(shift, cells, place, bit):
    residue = shift & (cells - 1)
    hops = shift >> log2(cells)
    near = ((place - hops) ^ place) & bit
    far = ((place - hops - 1) ^ place) & bit
    lane = iota((8, LANES), 1)
    return [jnp.where(lane + j * LANES < cells - residue, near, far) != 0 for j in range(2)]


def select_kernel(bit, shifts_ref, kept_ref, came_ref, coeffs_ref, out_ref, later_ref):
    later_ref[...] = coeffs_ref[...]
    rows = shifts_ref.shape[0]
    place = lax.axis_index("az")
    for batch in range(0, rows, BATCH):
        values = []
        for r in range(batch, batch + BATCH):
            take = masks(shifts_ref[r], 2 * LANES, place, bit)
            values.append([jnp.where(take[j], came_ref[r, j], kept_ref[r, j]) for j in range(2)])
        for r, value in zip(range(batch, batch + BATCH), values):
            for j in range(2):
                out_ref[r, j] = value[j]
    out_ref[rows:] = kept_ref[rows:] + came_ref[rows:]


def turned(value, residue):
    amount = residue & (LANES - 1)
    low = iota(value[0].shape, 1) < amount
    turn = [pltpu.roll(x, amount, 1) for x in value]
    return [jnp.where(low, turn[1], turn[0]), jnp.where(low, turn[0], turn[1])]


def rotate_kernel(count, bit, shifts_ref, kept_ref, came_ref, out_ref, ghosts_ref):
    rows, tiles, fields, lanes = out_ref.shape
    cells = tiles * lanes
    per_tile = lanes // (2 * rows)
    place = lax.axis_index("az")
    lane = iota((fields, lanes), 1)
    for at in range(count * 2 * rows // lanes):
        ghosts_ref[at] = kept_ref[rows + at // 2, at % 2] + came_ref[rows + at // 2, at % 2]
    for batch in range(0, rows, BATCH):
        values = []
        for r in range(batch, batch + BATCH):
            shift = shifts_ref[r]
            hops = shift >> log2(cells)
            residue = shift & (cells - 1)
            take = masks(shift, cells, place, bit)
            value = [jnp.where(take[j], came_ref[r, j], kept_ref[r, j]) for j in range(2)]
            here = (place - hops) & (count - 1)
            before = (here - 1) & (count - 1)
            after = jnp.where(residue > 0, here, (here + 1) & (count - 1))
            low_at = (before & (per_tile - 1)) * 2 * rows + r
            high_at = (after & (per_tile - 1)) * 2 * rows + rows + r
            low = pltpu.roll(ghosts_ref[before >> log2(per_tile)], (lanes - low_at) & (lanes - 1), 1)
            high = pltpu.roll(ghosts_ref[after >> log2(per_tile)], lanes - 1 - high_at, 1)
            value[0] = value[0] + jnp.where(lane == 0, low, 0.0)
            value[1] = value[1] + jnp.where(lane == lanes - 1, high, 0.0)
            values.append((r, residue >> log2(lanes), turned(value, residue)))
        for r, swap, value in values:
            out_ref[r, swap] = value[0]
            out_ref[r, 1 - swap] = value[1]


def finish_kernel(count, starts, shifts_ref, columns_ref, rotated_ref, *rest):
    out_hbm, forcing_ref, total_ref, sems = rest[len(starts) :]
    rows, tiles, fields, lanes = rotated_ref.shape
    cells = tiles * lanes
    place = lax.axis_index("az")
    lane = iota((fields, lanes), 1)
    for at, part in zip(reversed(starts), rest):
        forcing_ref[at : at + part.shape[0]] = part[...]
    for m in range(count):
        before = (((place ^ m) - 1) & (count - 1)) ^ place
        after = (((place ^ m) + 1) & (count - 1)) ^ place
        for e in range(2):
            forcing_ref[m, e, 0] += jnp.where(lane == 0, forcing_ref[before, e, tiles], 0.0)
            forcing_ref[m, e, 1] += jnp.where(lane == lanes - 1, forcing_ref[after, e, tiles], 0.0)
    copies = []
    for batch in range(0, rows, BATCH):
        values = []
        for r in range(batch, batch + BATCH):
            shift = shifts_ref[r]
            hops = shift >> log2(cells)
            residue = shift & (cells - 1)
            here = (place - hops) & (count - 1)
            source = here ^ place
            source_low = ((here - 1) & (count - 1)) ^ place
            value = []
            for j in range(2):
                near = lane + j * lanes < cells - residue
                left = jnp.where(near, forcing_ref[source, 0, j], forcing_ref[source_low, 0, j])
                right = jnp.where(near, forcing_ref[source, 1, j], forcing_ref[source_low, 1, j])
                value.append(columns_ref[0, r] * left + columns_ref[1, r] * right)
            value = turned(value, residue)
            swap = residue >> log2(lanes)
            values.append(
                (swap, value[0] + rotated_ref[r, swap], value[1] + rotated_ref[r, 1 - swap])
            )
        at = batch // BATCH
        for i, (swap, near, far) in enumerate(values):
            total_ref[at, swap, pl.ds(i, fields, stride=BATCH), :] = near
            total_ref[at, 1 - swap, pl.ds(i, fields, stride=BATCH), :] = far
        for j in range(2):
            copies.append(
                pltpu.make_async_copy(
                    total_ref.at[at, j].reshape(fields, BATCH, lanes),
                    out_hbm.at[:, pl.ds(batch, BATCH), pl.ds(j * lanes, lanes)],
                    sems.at[at, j],
                )
            )
            copies[-1].start()
    for copy in copies:
        copy.wait()


def merge_kernel(level, count, first, *refs):
    refs = list(refs)
    own_ref, other_ref, coeffs_ref = refs[:3]
    sums_ref = None if first else refs[3]
    held_ref, sum_ref = refs[-2:] if not first else refs[5:7]
    place = lax.axis_index("rad")
    upper = iota((own_ref.shape[-2], LANES), 0) * 0 + (place & (1 << level)) != 0
    following = iota((own_ref.shape[-2], LANES), 0) * 0 + (place & (2 << level)) != 0
    q, own, other_scale, felt_l, felt_r, b, c = [coeffs_ref[7 * level + i] for i in range(7)]
    for t in range(own_ref.shape[1]):
        head, tail = own_ref[0, t], own_ref[1, t]
        meeting = jnp.where(upper, other_ref[1, t], other_ref[0, t])
        facing = jnp.where(upper, head, tail)
        inner = q * meeting + own * facing
        partner = q * facing + other_scale * meeting
        if first:
            sum_ref[0, t] = felt_l * inner
            sum_ref[1, t] = felt_r * inner
        else:
            sum_ref[0, t] = sums_ref[0, t] + felt_l * inner
            sum_ref[1, t] = sums_ref[1, t] + felt_r * inner
        head = jnp.where(upper, other_ref[0, t], head) + c * jnp.where(upper, partner, inner)
        tail = jnp.where(upper, tail, other_ref[1, t]) + b * jnp.where(upper, inner, partner)
        if 4 << level == count:
            held_ref[t] = jnp.where(following, head, tail)
        else:
            held_ref[0, t] = head
            held_ref[1, t] = tail


def merge(level, held, coeffs, extra):
    count = lax.axis_size("rad")
    first = level == 0
    last = 4 << level == count
    sums = pltpu.VMEM(held.shape, f32)
    message = pltpu.VMEM(held.shape[1:] if last else held.shape, f32)
    return pl.pallas_call(
        functools.partial(merge_kernel, level, count, first),
        out_shape=[pltpu.VMEM(extra.shape, f32), message, sums] if first else [message, sums],
        in_specs=[VMEM] * 4,
        out_specs=[VMEM] * (3 if first else 2),
        input_output_aliases={3: 0} if first else {},
        cost_estimate=cost(40000),
        name="merge",
    )(*map(in_vmem, (held, swapped(held, "rad", 1 << level), coeffs, extra)))


def join_kernel(own_ref, other_ref, coeffs_ref, sums_ref, out_ref):
    for e in range(2):
        for t in range(own_ref.shape[0]):
            out_ref[0, e, t] = (
                sums_ref[e, t]
                + coeffs_ref[2 * e] * other_ref[t]
                + coeffs_ref[2 * e + 1] * own_ref[t]
            )


def per_device(state, velocity, coupling, diffusivity, inverse, shifts):
    state = state[:, 0]
    fields, rows, cells = state.shape
    tiles = cells // LANES
    assert tiles == 2 and fields == 8 and 2 * rows <= LANES
    count = lax.axis_size("az")
    segments = lax.axis_size("rad")
    offsets, state_near, velocity, diffusivity, shifts, mixing = pl.pallas_call(
        offsets_kernel,
        out_shape=[
            pltpu.VMEM((2, tiles + 1, fields, LANES), f32),
            pltpu.VMEM(state.shape, f32),
            pltpu.VMEM((1, rows), f32),
            pltpu.VMEM((1, fields), f32),
            pltpu.SMEM(shifts.shape, jnp.int32),
            pltpu.SMEM(coupling.shape, f32),
        ],
        in_specs=[ANY] * 6,
        out_specs=[VMEM] * 4 + [SMEM] * 2,
        scratch_shapes=[
            pltpu.VMEM((fields, 8, rows), f32),
            pltpu.VMEM((fields, 8, rows), f32),
            pltpu.VMEM((fields, fields), f32),
            pltpu.SemaphoreType.DMA((8,)),
        ],
        cost_estimate=cost(5000),
        name="offsets",
    )(state, inverse, velocity[None], coupling, diffusivity[None], shifts)
    shifts = in_smem(shifts)
    spare = count * 2 * rows // cells
    solved, columns, coeffs, final = pl.pallas_call(
        functools.partial(solve_kernel, count, segments),
        out_shape=[
            pltpu.VMEM((rows + spare, tiles, fields, LANES), f32),
            pltpu.VMEM((2, rows, fields, LANES), f32),
            pltpu.VMEM((7 * log2(segments) - 7, fields, LANES), f32),
            pltpu.VMEM((4, fields, LANES), f32),
        ],
        in_specs=[SMEM] + [VMEM] * 4,
        out_specs=[VMEM] * 4,
        scratch_shapes=[
            pltpu.VMEM((fields, rows, cells), f32),
            pltpu.VMEM((fields * rows, cells + LANES), f32),
            pltpu.VMEM((fields * rows // LANES, fields * rows, LANES), f32),
        ],
        cost_estimate=cost(8000),
        name="solve",
    )(in_smem(mixing), *map(in_vmem, (state_near, velocity, diffusivity, inverse)))
    kept, held, sums = merge(0, offsets, coeffs, solved)
    bit = 1
    while 2 * bit < count:
        kept, coeffs = pl.pallas_call(
            functools.partial(select_kernel, bit),
            out_shape=[pltpu.VMEM(kept.shape, f32), pltpu.VMEM(coeffs.shape, f32)],
            in_specs=[SMEM] + [VMEM] * 3,
            out_specs=[VMEM] * 2,
            cost_estimate=cost(2800),
        name="select",
        )(shifts, in_vmem(kept), in_vmem(swapped(kept, "az", bit)), in_vmem(coeffs))
        bit *= 2
    rotated = pl.pallas_call(
        functools.partial(rotate_kernel, count, bit),
        out_shape=pltpu.VMEM((rows, tiles, fields, LANES), f32),
        in_specs=[SMEM] + [VMEM] * 2,
        out_specs=VMEM,
        scratch_shapes=[pltpu.VMEM((count * 2 * rows // LANES, fields, LANES), f32)],
        cost_estimate=cost(4000),
        name="rotate",
    )(shifts, in_vmem(kept), in_vmem(swapped(kept, "az", bit)))
    for level in range(1, log2(segments) - 1):
        held, sums = merge(level, held, coeffs, sums)
    forcing = pl.pallas_call(
        join_kernel,
        out_shape=pltpu.VMEM((1,) + sums.shape, f32),
        in_specs=[VMEM] * 4,
        out_specs=VMEM,
        cost_estimate=cost(400),
        name="join",
    )(*map(in_vmem, (held, swapped(held, "rad", segments // 2), final, sums)))
    parts = [forcing]
    bit = 1
    while bit < count:
        ours = parts[0] if len(parts) == 1 else jnp.concatenate(parts, 0)
        parts += [swapped(ours, "az", i * bit) for i in range(1, min(4, count // bit))]
        bit *= 4
    starts = [sum(x.shape[0] for x in parts[:i]) for i in range(len(parts))]
    out = pl.pallas_call(
        functools.partial(finish_kernel, count, starts),
        out_shape=jax.ShapeDtypeStruct(state.shape, f32),
        in_specs=[SMEM] + [VMEM] * (2 + len(parts)),
        out_specs=ANY,
        scratch_shapes=[
            pltpu.VMEM((count, 2, tiles + 1, fields, LANES), f32),
            pltpu.VMEM((rows // BATCH, tiles, BATCH * fields, LANES), f32),
            pltpu.SemaphoreType.DMA((rows // BATCH, tiles)),
        ],
        cost_estimate=cost(6000),
        name="finish",
    )(shifts, in_vmem(columns), in_vmem(rotated), *map(in_vmem, reversed(parts)))
    return out[:, None]


def solution(mesh):
    return jax.shard_map(
        per_device,
        mesh=mesh,
        in_specs=(P(None, None, "rad", "az"), P("rad"), P(), P(), P(), P("rad")),
        out_specs=P(None, None, "rad", "az"),
        check_vma=False,
    )
```

```python
import functools

import jax
import jax.numpy as jnp
from jax import lax
from jax.experimental import pallas as pl
from jax.experimental.pallas import tpu as pltpu
from jax.sharding import PartitionSpec as P

highest = lax.Precision.HIGHEST
f32 = jnp.float32
LANES = 128
BATCH = 8
SMEM = pl.BlockSpec(memory_space=pltpu.SMEM)
VMEM = pl.BlockSpec(memory_space=pltpu.VMEM)
ANY = pl.BlockSpec(memory_space=pl.ANY)


def cost(kilobytes):
    return pl.CostEstimate(flops=kilobytes << 18, bytes_accessed=kilobytes << 10, transcendentals=0)


def in_vmem(x):
    return pltpu.with_memory_space_constraint(x, pltpu.VMEM)


def in_smem(x):
    return pltpu.with_memory_space_constraint(x, pltpu.SMEM)


def iota(shape, dim):
    return lax.broadcasted_iota(jnp.int32, shape, dim)


def log2(number):
    assert number & (number - 1) == 0
    return number.bit_length() - 1


def swapped(block, axis, bit):
    return lax.ppermute(block, axis, [(i, i ^ bit) for i in range(lax.axis_size(axis))])


def tile(x, j):
    return x[:, j * LANES : (j + 1) * LANES]


def as_column(row):
    n = row.shape[1]
    same = iota((n, n), 0) == iota((n, n), 1)
    return jnp.sum(jnp.where(same, jnp.broadcast_to(row, (n, n)), 0.0), axis=1, keepdims=True)


def level_coefficients(first, last, count, place):
    fields = first.shape[0]
    wide = (fields, LANES)
    a = jnp.broadcast_to(first[:, :1], wide)
    b = jnp.broadcast_to(last[:, :1], wide)
    c = jnp.broadcast_to(first[:, -1:], wide)
    d = jnp.broadcast_to(last[:, -1:], wide)
    one, none = jnp.ones(wide, f32), jnp.zeros(wide, f32)
    left_l, left_r, right_l, right_r = one, none, none, one
    found = []
    bit = 1
    while bit < count:
        side = iota(wide, 0) * 0 + (place & bit)
        upper = side != 0
        q = 1.0 / (1.0 - a * d)
        own = q * jnp.where(upper, d, a)
        felt_l = jnp.where(upper, left_l, left_r)
        felt_r = jnp.where(upper, right_l, right_r)
        if 2 * bit == count:
            found += [felt_l * q, felt_l * own, felt_r * q, felt_r * own]
            break
        found += [q, own, q * jnp.where(upper, a, d), felt_l, felt_r, b, c]
        via_l = jnp.where(upper, b * q, a * b * q)
        via_r = jnp.where(upper, c * d * q, c * q)
        left_l, left_r = (
            jnp.where(upper, none, left_l) + felt_l * via_l,
            jnp.where(upper, left_r, none) + felt_l * via_r,
        )
        right_l, right_r = (
            jnp.where(upper, none, right_l) + felt_r * via_l,
            jnp.where(upper, right_r, none) + felt_r * via_r,
        )
        a, b, c, d = a + a * b * c * q, b * b * q, c * c * q, d + b * c * d * q
        bit *= 2
    return found


def offsets_kernel(
    state_hbm, inverse_hbm, velocity_hbm, coupling_hbm, diffusivity_hbm, shifts_hbm,
    out_ref, state_ref, velocity_ref, diffusivity_ref, shifts_ref, mixing_ref,
    first_ref, last_ref, coupling_ref, sems,
):
    fields, rows, cells = state_ref.shape
    copies = [
        pltpu.make_async_copy(source, target, sems.at[i])
        for i, (source, target) in enumerate(
            (
                (inverse_hbm.at[:, :8], first_ref),
                (inverse_hbm.at[:, rows - 8 :], last_ref),
                (coupling_hbm, coupling_ref),
                (velocity_hbm, velocity_ref),
                (diffusivity_hbm, diffusivity_ref),
                (state_hbm, state_ref),
                (shifts_hbm, shifts_ref),
                (coupling_hbm, mixing_ref),
            )
        )
    ]
    for copy in copies:
        copy.start()
    for copy in copies[:5]:
        copy.wait()
    span = fields * rows
    diffusivity = as_column(diffusivity_ref[...])
    first = diffusivity * first_ref[:, 0, :]
    last = diffusivity * last_ref[:, 7, :]
    first = jnp.concatenate([first] * fields, axis=1)
    last = jnp.concatenate([last] * fields, axis=1)
    speed = jnp.concatenate([jnp.broadcast_to(velocity_ref[...], (fields, rows))] * fields, axis=1)
    lane = iota((fields, span), 1)
    row = lane & (rows - 1)
    group = lane >> log2(rows)
    own = group == iota((fields, span), 0)
    mix = jnp.zeros((fields, span), f32)
    for g in range(fields):
        mix = jnp.where(group == g, coupling_ref[:, g : g + 1], mix)
    weights = []
    drift = []
    for vector, below, above in ((first, 1.0, 0.0), (last, 0.0, 1.0)):
        lower = jnp.where(row == 0, below, pltpu.roll(vector, 1, 1))
        upper = jnp.where(row == rows - 1, above, pltpu.roll(vector, span - 1, 1))
        weights.append(jnp.where(own, vector, 0.0) + 0.5 * mix * (lower - upper))
        drift.append(jnp.where(own, 0.5 * speed * vector, 0.0))
    table = jnp.concatenate(weights + drift, axis=0)
    copies[5].wait()
    sums = jnp.dot(
        table,
        state_ref[...].reshape(span, cells),
        precision=highest,
        preferred_element_type=f32,
    )
    blank = jnp.zeros((2 * fields, LANES), f32)
    main = jnp.concatenate([sums[: 2 * fields], blank], axis=1)
    side = jnp.concatenate([sums[2 * fields :], blank], axis=1)
    width = cells + LANES
    total = main + pltpu.roll(side, 1, 1) - pltpu.roll(side, width - 1, 1)
    for e in range(2):
        for j in range(width // LANES):
            out_ref[e, j] = tile(total[e * fields : (e + 1) * fields], j)
    for copy in copies[6:]:
        copy.wait()


def solve_kernel(
    count, segments, coupling_ref, state_ref, velocity_ref, diffusivity_ref, inverse_ref,
    out_ref, columns_ref, coeffs_ref, final_ref, diff_ref, updated_ref, table_ref,
):
    fields, rows, cells = state_ref.shape
    span = fields * rows
    width = cells + LANES
    row = iota((rows, cells), 0)
    half = 0.5 * as_column(velocity_ref[...])
    diffusivity = as_column(diffusivity_ref[...])
    first = diffusivity * inverse_ref[:, 0, :]
    last = diffusivity * inverse_ref[:, rows - 1, :]
    for i, x in enumerate(level_coefficients(first, last, segments, lax.axis_index("rad"))):
        if i < coeffs_ref.shape[0]:
            coeffs_ref[i] = x
        else:
            final_ref[i - coeffs_ref.shape[0]] = x
    for g in range(fields):
        block = state_ref[g]
        upper = jnp.where(row == rows - 1, 0.0, pltpu.roll(block, rows - 1, 0))
        lower = jnp.where(row == 0, 0.0, pltpu.roll(block, 1, 0))
        diff_ref[g] = 0.5 * (upper - lower)
        padded = jnp.concatenate([block, jnp.zeros((rows, LANES), f32)], axis=1)
        updated_ref[g * rows : (g + 1) * rows] = padded + half * (
            pltpu.roll(padded, 1, 1) - pltpu.roll(padded, width - 1, 1)
        )
        pad = [jnp.zeros((rows, rows), f32)] * fields
        pad[g] = inverse_ref[g]
        placed = jnp.concatenate(pad, axis=1)
        for j in range(span // LANES):
            table_ref[j, pl.ds(g, rows, stride=fields), :] = tile(placed, j)
    for f in range(fields):
        total = updated_ref[f * rows : (f + 1) * rows, :cells]
        for g in range(fields):
            total = total + coupling_ref[f, g] * diff_ref[g]
        updated_ref[f * rows : (f + 1) * rows, :cells] = total
    solved = jnp.dot(
        jnp.concatenate([table_ref[j] for j in range(span // LANES)], axis=1),
        updated_ref[...],
        precision=highest,
        preferred_element_type=f32,
    )
    lane = iota((fields, LANES), 1)
    ghosts = jnp.zeros((fields, LANES), f32)
    for r in range(rows):
        block = solved[r * fields : (r + 1) * fields]
        out_ref[r, 0] = tile(block, 0)
        out_ref[r, 1] = tile(block, 1)
        edge = tile(block, 2)
        ghosts = jnp.where(lane == r, pltpu.roll(edge, r, 1), ghosts)
        ghosts = jnp.where(lane == rows + r, pltpu.roll(edge, rows + r + 1, 1), ghosts)
        columns_ref[0, r] = jnp.broadcast_to(inverse_ref[:, r, :1], (fields, LANES))
        columns_ref[1, r] = jnp.broadcast_to(inverse_ref[:, r, rows - 1 :], (fields, LANES))
    place = lax.axis_index("az")
    for at in range(count * 2 * rows // LANES):
        for part in range(LANES // (2 * rows)):
            mine = iota((fields, LANES), 0) * 0 + place == at * (LANES // (2 * rows)) + part
            moved = pltpu.roll(ghosts, part * 2 * rows, 1) if part else ghosts
            value = jnp.where(mine, moved, 0.0)
            total = value if part == 0 else total + value
        out_ref[rows + at // 2, at % 2] = total


def masks(shift, cells, place, bit):
    residue = shift & (cells - 1)
    hops = shift >> log2(cells)
    near = ((place - hops) ^ place) & bit
    far = ((place - hops - 1) ^ place) & bit
    lane = iota((8, LANES), 1)
    return [jnp.where(lane + j * LANES < cells - residue, near, far) != 0 for j in range(2)]


def select_kernel(bit, shifts_ref, kept_ref, came_ref, coeffs_ref, out_ref, later_ref):
    later_ref[...] = coeffs_ref[...]
    rows = shifts_ref.shape[0]
    place = lax.axis_index("az")
    for batch in range(0, rows, BATCH):
        values = []
        for r in range(batch, batch + BATCH):
            take = masks(shifts_ref[r], 2 * LANES, place, bit)
            values.append([jnp.where(take[j], came_ref[r, j], kept_ref[r, j]) for j in range(2)])
        for r, value in zip(range(batch, batch + BATCH), values):
            for j in range(2):
                out_ref[r, j] = value[j]
    out_ref[rows:] = kept_ref[rows:] + came_ref[rows:]


def turned(value, residue):
    amount = residue & (LANES - 1)
    low = iota(value[0].shape, 1) < amount
    turn = [pltpu.roll(x, amount, 1) for x in value]
    return [jnp.where(low, turn[1], turn[0]), jnp.where(low, turn[0], turn[1])]


def rotate_kernel(count, bit, shifts_ref, kept_ref, came_ref, out_ref, ghosts_ref):
    rows, tiles, fields, lanes = out_ref.shape
    cells = tiles * lanes
    per_tile = lanes // (2 * rows)
    place = lax.axis_index("az")
    lane = iota((fields, lanes), 1)
    for at in range(count * 2 * rows // lanes):
        ghosts_ref[at] = kept_ref[rows + at // 2, at % 2] + came_ref[rows + at // 2, at % 2]
    for batch in range(0, rows, BATCH):
        values = []
        for r in range(batch, batch + BATCH):
            shift = shifts_ref[r]
            hops = shift >> log2(cells)
            residue = shift & (cells - 1)
            take = masks(shift, cells, place, bit)
            value = [jnp.where(take[j], came_ref[r, j], kept_ref[r, j]) for j in range(2)]
            here = (place - hops) & (count - 1)
            before = (here - 1) & (count - 1)
            after = jnp.where(residue > 0, here, (here + 1) & (count - 1))
            low_at = (before & (per_tile - 1)) * 2 * rows + r
            high_at = (after & (per_tile - 1)) * 2 * rows + rows + r
            low = pltpu.roll(ghosts_ref[before >> log2(per_tile)], (lanes - low_at) & (lanes - 1), 1)
            high = pltpu.roll(ghosts_ref[after >> log2(per_tile)], lanes - 1 - high_at, 1)
            value[0] = value[0] + jnp.where(lane == 0, low, 0.0)
            value[1] = value[1] + jnp.where(lane == lanes - 1, high, 0.0)
            values.append((r, residue >> log2(lanes), turned(value, residue)))
        for r, swap, value in values:
            out_ref[r, swap] = value[0]
            out_ref[r, 1 - swap] = value[1]


def finish_kernel(count, starts, shifts_ref, columns_ref, rotated_ref, *rest):
    out_hbm, ghosts_ref, forcing_ref, total_ref, sems = rest[len(starts) :]
    rows, tiles, fields, lanes = rotated_ref.shape
    cells = tiles * lanes
    place = lax.axis_index("az")
    lane = iota((fields, lanes), 1)
    for at, part in zip(reversed(starts), rest):
        ghosts_ref[at : at + part.shape[0]] = part[:, :, tiles]
    for at, part in zip(reversed(starts), rest):
        for i in range(part.shape[0]):
            own = place ^ (at + i)
            before = ((own - 1) & (count - 1)) ^ place
            after = ((own + 1) & (count - 1)) ^ place
            for e in range(2):
                low = jnp.where(lane == 0, ghosts_ref[before, e], 0.0)
                high = jnp.where(lane == lanes - 1, ghosts_ref[after, e], 0.0)
                forcing_ref[at + i, e, 0] = part[i, e, 0] + low
                forcing_ref[at + i, e, 1] = part[i, e, 1] + high
    copies = []
    for batch in range(0, rows, BATCH):
        values = []
        for r in range(batch, batch + BATCH):
            shift = shifts_ref[r]
            hops = shift >> log2(cells)
            residue = shift & (cells - 1)
            here = (place - hops) & (count - 1)
            source = here ^ place
            source_low = ((here - 1) & (count - 1)) ^ place
            value = []
            for j in range(2):
                near = lane + j * lanes < cells - residue
                left = jnp.where(near, forcing_ref[source, 0, j], forcing_ref[source_low, 0, j])
                right = jnp.where(near, forcing_ref[source, 1, j], forcing_ref[source_low, 1, j])
                value.append(columns_ref[0, r] * left + columns_ref[1, r] * right)
            value = turned(value, residue)
            swap = residue >> log2(lanes)
            values.append(
                (swap, value[0] + rotated_ref[r, swap], value[1] + rotated_ref[r, 1 - swap])
            )
        at = batch // BATCH
        for i, (swap, near, far) in enumerate(values):
            total_ref[at, swap, pl.ds(i, fields, stride=BATCH), :] = near
            total_ref[at, 1 - swap, pl.ds(i, fields, stride=BATCH), :] = far
        for j in range(2):
            copies.append(
                pltpu.make_async_copy(
                    total_ref.at[at, j].reshape(fields, BATCH, lanes),
                    out_hbm.at[:, pl.ds(batch, BATCH), pl.ds(j * lanes, lanes)],
                    sems.at[at, j],
                )
            )
            copies[-1].start()
    for copy in copies:
        copy.wait()


def merge_kernel(level, count, first, *refs):
    refs = list(refs)
    own_ref, other_ref, coeffs_ref = refs[:3]
    sums_ref = None if first else refs[3]
    held_ref, sum_ref = refs[-2:] if not first else refs[5:7]
    place = lax.axis_index("rad")
    upper = iota((own_ref.shape[-2], LANES), 0) * 0 + (place & (1 << level)) != 0
    following = iota((own_ref.shape[-2], LANES), 0) * 0 + (place & (2 << level)) != 0
    q, own, other_scale, felt_l, felt_r, b, c = [coeffs_ref[7 * level + i] for i in range(7)]
    for t in range(own_ref.shape[1]):
        head, tail = own_ref[0, t], own_ref[1, t]
        meeting = jnp.where(upper, other_ref[1, t], other_ref[0, t])
        facing = jnp.where(upper, head, tail)
        inner = q * meeting + own * facing
        partner = q * facing + other_scale * meeting
        if first:
            sum_ref[0, t] = felt_l * inner
            sum_ref[1, t] = felt_r * inner
        else:
            sum_ref[0, t] = sums_ref[0, t] + felt_l * inner
            sum_ref[1, t] = sums_ref[1, t] + felt_r * inner
        head = jnp.where(upper, other_ref[0, t], head) + c * jnp.where(upper, partner, inner)
        tail = jnp.where(upper, tail, other_ref[1, t]) + b * jnp.where(upper, inner, partner)
        if 4 << level == count:
            held_ref[t] = jnp.where(following, head, tail)
        else:
            held_ref[0, t] = head
            held_ref[1, t] = tail


def merge(level, held, coeffs, extra):
    count = lax.axis_size("rad")
    first = level == 0
    last = 4 << level == count
    sums = pltpu.VMEM(held.shape, f32)
    message = pltpu.VMEM(held.shape[1:] if last else held.shape, f32)
    return pl.pallas_call(
        functools.partial(merge_kernel, level, count, first),
        out_shape=[pltpu.VMEM(extra.shape, f32), message, sums] if first else [message, sums],
        in_specs=[VMEM] * 4,
        out_specs=[VMEM] * (3 if first else 2),
        input_output_aliases={3: 0} if first else {},
        cost_estimate=cost(40000),
        name="merge",
    )(*map(in_vmem, (held, swapped(held, "rad", 1 << level), coeffs, extra)))


def join_kernel(own_ref, other_ref, coeffs_ref, sums_ref, out_ref):
    for e in range(2):
        for t in range(own_ref.shape[0]):
            out_ref[0, e, t] = (
                sums_ref[e, t]
                + coeffs_ref[2 * e] * other_ref[t]
                + coeffs_ref[2 * e + 1] * own_ref[t]
            )


def per_device(state, velocity, coupling, diffusivity, inverse, shifts):
    state = state[:, 0]
    fields, rows, cells = state.shape
    tiles = cells // LANES
    assert tiles == 2 and fields == 8 and 2 * rows <= LANES
    count = lax.axis_size("az")
    segments = lax.axis_size("rad")
    offsets, state_near, velocity, diffusivity, shifts, mixing = pl.pallas_call(
        offsets_kernel,
        out_shape=[
            pltpu.VMEM((2, tiles + 1, fields, LANES), f32),
            pltpu.VMEM(state.shape, f32),
            pltpu.VMEM((1, rows), f32),
            pltpu.VMEM((1, fields), f32),
            pltpu.SMEM(shifts.shape, jnp.int32),
            pltpu.SMEM(coupling.shape, f32),
        ],
        in_specs=[ANY] * 6,
        out_specs=[VMEM] * 4 + [SMEM] * 2,
        scratch_shapes=[
            pltpu.VMEM((fields, 8, rows), f32),
            pltpu.VMEM((fields, 8, rows), f32),
            pltpu.VMEM((fields, fields), f32),
            pltpu.SemaphoreType.DMA((8,)),
        ],
        cost_estimate=cost(5000),
        name="offsets",
    )(state, inverse, velocity[None], coupling, diffusivity[None], shifts)
    shifts = in_smem(shifts)
    spare = -(-count * 2 * rows // cells)
    solved, columns, coeffs, final = pl.pallas_call(
        functools.partial(solve_kernel, count, segments),
        out_shape=[
            pltpu.VMEM((rows + spare, tiles, fields, LANES), f32),
            pltpu.VMEM((2, rows, fields, LANES), f32),
            pltpu.VMEM((7 * log2(segments) - 7, fields, LANES), f32),
            pltpu.VMEM((4, fields, LANES), f32),
        ],
        in_specs=[SMEM] + [VMEM] * 4,
        out_specs=[VMEM] * 4,
        scratch_shapes=[
            pltpu.VMEM((fields, rows, cells), f32),
            pltpu.VMEM((fields * rows, cells + LANES), f32),
            pltpu.VMEM((fields * rows // LANES, fields * rows, LANES), f32),
        ],
        cost_estimate=cost(8000),
        name="solve",
    )(in_smem(mixing), *map(in_vmem, (state_near, velocity, diffusivity, inverse)))
    kept, held, sums = merge(0, offsets, coeffs, solved)
    bit = 1
    while 2 * bit < count:
        kept, coeffs = pl.pallas_call(
            functools.partial(select_kernel, bit),
            out_shape=[pltpu.VMEM(kept.shape, f32), pltpu.VMEM(coeffs.shape, f32)],
            in_specs=[SMEM] + [VMEM] * 3,
            out_specs=[VMEM] * 2,
            cost_estimate=cost(2800),
        name="select",
        )(shifts, in_vmem(kept), in_vmem(swapped(kept, "az", bit)), in_vmem(coeffs))
        bit *= 2
    rotated = pl.pallas_call(
        functools.partial(rotate_kernel, count, bit),
        out_shape=pltpu.VMEM((rows, tiles, fields, LANES), f32),
        in_specs=[SMEM] + [VMEM] * 2,
        out_specs=VMEM,
        scratch_shapes=[pltpu.VMEM((count * 2 * rows // LANES, fields, LANES), f32)],
        cost_estimate=cost(4000),
        name="rotate",
    )(shifts, in_vmem(kept), in_vmem(swapped(kept, "az", bit)))
    for level in range(1, log2(segments) - 1):
        held, sums = merge(level, held, coeffs, sums)
    forcing = pl.pallas_call(
        join_kernel,
        out_shape=pltpu.VMEM((1,) + sums.shape, f32),
        in_specs=[VMEM] * 4,
        out_specs=VMEM,
        cost_estimate=cost(400),
        name="join",
    )(*map(in_vmem, (held, swapped(held, "rad", segments // 2), final, sums)))
    parts = [forcing]
    bit = 1
    while bit < count:
        ours = parts[0] if len(parts) == 1 else jnp.concatenate(parts, 0)
        parts += [swapped(ours, "az", i * bit) for i in range(1, min(4, count // bit))]
        bit *= 4
    starts = [sum(x.shape[0] for x in parts[:i]) for i in range(len(parts))]
    out = pl.pallas_call(
        functools.partial(finish_kernel, count, starts),
        out_shape=jax.ShapeDtypeStruct(state.shape, f32),
        in_specs=[SMEM] + [VMEM] * (2 + len(parts)),
        out_specs=ANY,
        scratch_shapes=[
            pltpu.VMEM((count, 2, fields, LANES), f32),
            pltpu.VMEM((count, 2, tiles, fields, LANES), f32),
            pltpu.VMEM((rows // BATCH, tiles, BATCH * fields, LANES), f32),
            pltpu.SemaphoreType.DMA((rows // BATCH, tiles)),
        ],
        cost_estimate=cost(6000),
        name="finish",
    )(shifts, in_vmem(columns), in_vmem(rotated), *map(in_vmem, reversed(parts)))
    return out[:, None]


def solution(mesh):
    return jax.shard_map(
        per_device,
        mesh=mesh,
        in_specs=(P(None, None, "rad", "az"), P("rad"), P(), P(), P(), P("rad")),
        out_specs=P(None, None, "rad", "az"),
        check_vma=False,
    )
```

```python
import functools

import jax
import jax.numpy as jnp
from jax import lax
from jax.experimental import pallas as pl
from jax.experimental.pallas import tpu as pltpu
from jax.sharding import PartitionSpec as P

highest = lax.Precision.HIGHEST
f32 = jnp.float32
LANES = 128
BATCH = 8
SMEM = pl.BlockSpec(memory_space=pltpu.SMEM)
VMEM = pl.BlockSpec(memory_space=pltpu.VMEM)
ANY = pl.BlockSpec(memory_space=pl.ANY)


def cost(kilobytes):
    return pl.CostEstimate(flops=kilobytes << 18, bytes_accessed=kilobytes << 10, transcendentals=0)


def in_vmem(x):
    return pltpu.with_memory_space_constraint(x, pltpu.VMEM)


def in_smem(x):
    return pltpu.with_memory_space_constraint(x, pltpu.SMEM)


def iota(shape, dim):
    return lax.broadcasted_iota(jnp.int32, shape, dim)


def log2(number):
    assert number & (number - 1) == 0
    return number.bit_length() - 1


def swapped(block, axis, bit):
    return lax.ppermute(block, axis, [(i, i ^ bit) for i in range(lax.axis_size(axis))])


def tile(x, j):
    return x[:, j * LANES : (j + 1) * LANES]


def as_column(row):
    n = row.shape[1]
    same = iota((n, n), 0) == iota((n, n), 1)
    return jnp.sum(jnp.where(same, jnp.broadcast_to(row, (n, n)), 0.0), axis=1, keepdims=True)


def level_coefficients(first, last, count, place):
    fields = first.shape[0]
    wide = (fields, LANES)
    a = jnp.broadcast_to(first[:, :1], wide)
    b = jnp.broadcast_to(last[:, :1], wide)
    c = jnp.broadcast_to(first[:, -1:], wide)
    d = jnp.broadcast_to(last[:, -1:], wide)
    one, none = jnp.ones(wide, f32), jnp.zeros(wide, f32)
    left_l, left_r, right_l, right_r = one, none, none, one
    found = []
    bit = 1
    while bit < count:
        side = iota(wide, 0) * 0 + (place & bit)
        upper = side != 0
        q = 1.0 / (1.0 - a * d)
        own = q * jnp.where(upper, d, a)
        felt_l = jnp.where(upper, left_l, left_r)
        felt_r = jnp.where(upper, right_l, right_r)
        if 2 * bit == count:
            found += [felt_l * q, felt_l * own, felt_r * q, felt_r * own]
            break
        found += [q, own, q * jnp.where(upper, a, d), felt_l, felt_r, b, c]
        via_l = jnp.where(upper, b * q, a * b * q)
        via_r = jnp.where(upper, c * d * q, c * q)
        left_l, left_r = (
            jnp.where(upper, none, left_l) + felt_l * via_l,
            jnp.where(upper, left_r, none) + felt_l * via_r,
        )
        right_l, right_r = (
            jnp.where(upper, none, right_l) + felt_r * via_l,
            jnp.where(upper, right_r, none) + felt_r * via_r,
        )
        a, b, c, d = a + a * b * c * q, b * b * q, c * c * q, d + b * c * d * q
        bit *= 2
    return found


def offsets_kernel(
    state_hbm, inverse_hbm, velocity_hbm, coupling_hbm, diffusivity_hbm, shifts_hbm,
    out_ref, state_ref, velocity_ref, diffusivity_ref, shifts_ref, mixing_ref,
    first_ref, last_ref, coupling_ref, sems,
):
    fields, rows, cells = state_ref.shape
    copies = [
        pltpu.make_async_copy(source, target, sems.at[i])
        for i, (source, target) in enumerate(
            (
                (inverse_hbm.at[:, :8], first_ref),
                (inverse_hbm.at[:, rows - 8 :], last_ref),
                (coupling_hbm, coupling_ref),
                (velocity_hbm, velocity_ref),
                (diffusivity_hbm, diffusivity_ref),
                (state_hbm, state_ref),
                (shifts_hbm, shifts_ref),
                (coupling_hbm, mixing_ref),
            )
        )
    ]
    for copy in copies:
        copy.start()
    for copy in copies[:5]:
        copy.wait()
    span = fields * rows
    diffusivity = as_column(diffusivity_ref[...])
    first = diffusivity * first_ref[:, 0, :]
    last = diffusivity * last_ref[:, 7, :]
    first = jnp.concatenate([first] * fields, axis=1)
    last = jnp.concatenate([last] * fields, axis=1)
    speed = jnp.concatenate([jnp.broadcast_to(velocity_ref[...], (fields, rows))] * fields, axis=1)
    lane = iota((fields, span), 1)
    row = lane & (rows - 1)
    group = lane >> log2(rows)
    own = group == iota((fields, span), 0)
    mix = jnp.zeros((fields, span), f32)
    for g in range(fields):
        mix = jnp.where(group == g, coupling_ref[:, g : g + 1], mix)
    weights = []
    drift = []
    for vector, below, above in ((first, 1.0, 0.0), (last, 0.0, 1.0)):
        lower = jnp.where(row == 0, below, pltpu.roll(vector, 1, 1))
        upper = jnp.where(row == rows - 1, above, pltpu.roll(vector, span - 1, 1))
        weights.append(jnp.where(own, vector, 0.0) + 0.5 * mix * (lower - upper))
        drift.append(jnp.where(own, 0.5 * speed * vector, 0.0))
    table = jnp.concatenate(weights + drift, axis=0)
    copies[5].wait()
    sums = jnp.dot(
        table,
        state_ref[...].reshape(span, cells),
        precision=highest,
        preferred_element_type=f32,
    )
    blank = jnp.zeros((2 * fields, LANES), f32)
    main = jnp.concatenate([sums[: 2 * fields], blank], axis=1)
    side = jnp.concatenate([sums[2 * fields :], blank], axis=1)
    width = cells + LANES
    total = main + pltpu.roll(side, 1, 1) - pltpu.roll(side, width - 1, 1)
    for e in range(2):
        for j in range(width // LANES):
            out_ref[e, j] = tile(total[e * fields : (e + 1) * fields], j)
    for copy in copies[6:]:
        copy.wait()


def solve_kernel(
    count, segments, coupling_ref, state_ref, velocity_ref, diffusivity_ref, inverse_ref,
    out_ref, columns_ref, coeffs_ref, final_ref, diff_ref, updated_ref, table_ref,
):
    fields, rows, cells = state_ref.shape
    span = fields * rows
    width = cells + LANES
    row = iota((rows, cells), 0)
    half = 0.5 * as_column(velocity_ref[...])
    diffusivity = as_column(diffusivity_ref[...])
    first = diffusivity * inverse_ref[:, 0, :]
    last = diffusivity * inverse_ref[:, rows - 1, :]
    for i, x in enumerate(level_coefficients(first, last, segments, lax.axis_index("rad"))):
        if i < coeffs_ref.shape[0]:
            coeffs_ref[i] = x
        else:
            final_ref[i - coeffs_ref.shape[0]] = x
    for g in range(fields):
        block = state_ref[g]
        upper = jnp.where(row == rows - 1, 0.0, pltpu.roll(block, rows - 1, 0))
        lower = jnp.where(row == 0, 0.0, pltpu.roll(block, 1, 0))
        diff_ref[g] = 0.5 * (upper - lower)
        padded = jnp.concatenate([block, jnp.zeros((rows, LANES), f32)], axis=1)
        updated_ref[g * rows : (g + 1) * rows] = padded + half * (
            pltpu.roll(padded, 1, 1) - pltpu.roll(padded, width - 1, 1)
        )
        pad = [jnp.zeros((rows, rows), f32)] * fields
        pad[g] = inverse_ref[g]
        placed = jnp.concatenate(pad, axis=1)
        for j in range(span // LANES):
            table_ref[j, pl.ds(g, rows, stride=fields), :] = tile(placed, j)
    for f in range(fields):
        total = updated_ref[f * rows : (f + 1) * rows, :cells]
        for g in range(fields):
            total = total + coupling_ref[f, g] * diff_ref[g]
        updated_ref[f * rows : (f + 1) * rows, :cells] = total
    solved = jnp.dot(
        jnp.concatenate([table_ref[j] for j in range(span // LANES)], axis=1),
        updated_ref[...],
        precision=highest,
        preferred_element_type=f32,
    )
    lane = iota((fields, LANES), 1)
    ghosts = jnp.zeros((fields, LANES), f32)
    for r in range(rows):
        block = solved[r * fields : (r + 1) * fields]
        out_ref[r, 0] = tile(block, 0)
        out_ref[r, 1] = tile(block, 1)
        edge = tile(block, 2)
        ghosts = jnp.where(lane == r, pltpu.roll(edge, r, 1), ghosts)
        ghosts = jnp.where(lane == rows + r, pltpu.roll(edge, rows + r + 1, 1), ghosts)
        columns_ref[0, r] = jnp.broadcast_to(inverse_ref[:, r, :1], (fields, LANES))
        columns_ref[1, r] = jnp.broadcast_to(inverse_ref[:, r, rows - 1 :], (fields, LANES))
    place = lax.axis_index("az")
    for at in range(count * 2 * rows // LANES):
        for part in range(LANES // (2 * rows)):
            mine = iota((fields, LANES), 0) * 0 + place == at * (LANES // (2 * rows)) + part
            moved = pltpu.roll(ghosts, part * 2 * rows, 1) if part else ghosts
            value = jnp.where(mine, moved, 0.0)
            total = value if part == 0 else total + value
        out_ref[rows + at // 2, at % 2] = total


def masks(shift, cells, place, bit):
    residue = shift & (cells - 1)
    hops = shift >> log2(cells)
    near = ((place - hops) ^ place) & bit
    far = ((place - hops - 1) ^ place) & bit
    lane = iota((8, LANES), 1)
    return [jnp.where(lane + j * LANES < cells - residue, near, far) != 0 for j in range(2)]


def select_kernel(bit, shifts_ref, kept_ref, came_ref, coeffs_ref, out_ref, later_ref):
    later_ref[...] = coeffs_ref[...]
    rows = shifts_ref.shape[0]
    place = lax.axis_index("az")
    for batch in range(0, rows, BATCH):
        values = []
        for r in range(batch, batch + BATCH):
            take = masks(shifts_ref[r], 2 * LANES, place, bit)
            values.append([jnp.where(take[j], came_ref[r, j], kept_ref[r, j]) for j in range(2)])
        for r, value in zip(range(batch, batch + BATCH), values):
            for j in range(2):
                out_ref[r, j] = value[j]
    out_ref[rows:] = kept_ref[rows:] + came_ref[rows:]


def turned(value, residue):
    amount = residue & (LANES - 1)
    low = iota(value[0].shape, 1) < amount
    turn = [pltpu.roll(x, amount, 1) for x in value]
    return [jnp.where(low, turn[1], turn[0]), jnp.where(low, turn[0], turn[1])]


def rotate_kernel(count, bit, shifts_ref, kept_ref, came_ref, out_ref, ghosts_ref):
    rows, tiles, fields, lanes = out_ref.shape
    cells = tiles * lanes
    per_tile = lanes // (2 * rows)
    place = lax.axis_index("az")
    lane = iota((fields, lanes), 1)
    for at in range(count * 2 * rows // lanes):
        ghosts_ref[at] = kept_ref[rows + at // 2, at % 2] + came_ref[rows + at // 2, at % 2]
    for batch in range(0, rows, BATCH):
        values = []
        for r in range(batch, batch + BATCH):
            shift = shifts_ref[r]
            hops = shift >> log2(cells)
            residue = shift & (cells - 1)
            take = masks(shift, cells, place, bit)
            value = [jnp.where(take[j], came_ref[r, j], kept_ref[r, j]) for j in range(2)]
            here = (place - hops) & (count - 1)
            before = (here - 1) & (count - 1)
            after = jnp.where(residue > 0, here, (here + 1) & (count - 1))
            low_at = (before & (per_tile - 1)) * 2 * rows + r
            high_at = (after & (per_tile - 1)) * 2 * rows + rows + r
            low = pltpu.roll(ghosts_ref[before >> log2(per_tile)], (lanes - low_at) & (lanes - 1), 1)
            high = pltpu.roll(ghosts_ref[after >> log2(per_tile)], lanes - 1 - high_at, 1)
            value[0] = value[0] + jnp.where(lane == 0, low, 0.0)
            value[1] = value[1] + jnp.where(lane == lanes - 1, high, 0.0)
            values.append((r, residue >> log2(lanes), turned(value, residue)))
        for r, swap, value in values:
            out_ref[r, swap] = value[0]
            out_ref[r, 1 - swap] = value[1]


def finish_kernel(count, starts, shifts_ref, columns_ref, rotated_ref, *rest):
    out_hbm, ghosts_ref, forcing_ref, total_ref, sems = rest[len(starts) :]
    rows, tiles, fields, lanes = rotated_ref.shape
    cells = tiles * lanes
    place = lax.axis_index("az")
    lane = iota((fields, lanes), 1)
    for at, part in zip(reversed(starts), rest):
        for i in range(part.shape[0]):
            packed = part[i, 2 * tiles]
            ghosts_ref[at + i, 0] = packed
            ghosts_ref[at + i, 1] = pltpu.roll(packed, lanes // 2, 1)
    for at, part in zip(reversed(starts), rest):
        for i in range(part.shape[0]):
            own = place ^ (at + i)
            before = ((own - 1) & (count - 1)) ^ place
            after = ((own + 1) & (count - 1)) ^ place
            for e in range(2):
                low = jnp.where(lane == 0, ghosts_ref[before, e], 0.0)
                high = jnp.where(lane == lanes - 1, ghosts_ref[after, e], 0.0)
                forcing_ref[at + i, e, 0] = part[i, tiles * e] + low
                forcing_ref[at + i, e, 1] = part[i, tiles * e + 1] + high
    copies = []
    for batch in range(0, rows, BATCH):
        values = []
        for r in range(batch, batch + BATCH):
            shift = shifts_ref[r]
            hops = shift >> log2(cells)
            residue = shift & (cells - 1)
            here = (place - hops) & (count - 1)
            source = here ^ place
            source_low = ((here - 1) & (count - 1)) ^ place
            value = []
            for j in range(2):
                near = lane + j * lanes < cells - residue
                left = jnp.where(near, forcing_ref[source, 0, j], forcing_ref[source_low, 0, j])
                right = jnp.where(near, forcing_ref[source, 1, j], forcing_ref[source_low, 1, j])
                value.append(columns_ref[0, r] * left + columns_ref[1, r] * right)
            value = turned(value, residue)
            swap = residue >> log2(lanes)
            values.append(
                (swap, value[0] + rotated_ref[r, swap], value[1] + rotated_ref[r, 1 - swap])
            )
        at = batch // BATCH
        for i, (swap, near, far) in enumerate(values):
            total_ref[at, swap, pl.ds(i, fields, stride=BATCH), :] = near
            total_ref[at, 1 - swap, pl.ds(i, fields, stride=BATCH), :] = far
        for j in range(2):
            copies.append(
                pltpu.make_async_copy(
                    total_ref.at[at, j].reshape(fields, BATCH, lanes),
                    out_hbm.at[:, pl.ds(batch, BATCH), pl.ds(j * lanes, lanes)],
                    sems.at[at, j],
                )
            )
            copies[-1].start()
    for copy in copies:
        copy.wait()


def merge_kernel(level, count, first, *refs):
    refs = list(refs)
    own_ref, other_ref, coeffs_ref = refs[:3]
    sums_ref = None if first else refs[3]
    held_ref, sum_ref = refs[-2:] if not first else refs[5:7]
    place = lax.axis_index("rad")
    upper = iota((own_ref.shape[-2], LANES), 0) * 0 + (place & (1 << level)) != 0
    following = iota((own_ref.shape[-2], LANES), 0) * 0 + (place & (2 << level)) != 0
    q, own, other_scale, felt_l, felt_r, b, c = [coeffs_ref[7 * level + i] for i in range(7)]
    for t in range(own_ref.shape[1]):
        head, tail = own_ref[0, t], own_ref[1, t]
        meeting = jnp.where(upper, other_ref[1, t], other_ref[0, t])
        facing = jnp.where(upper, head, tail)
        inner = q * meeting + own * facing
        partner = q * facing + other_scale * meeting
        if first:
            sum_ref[0, t] = felt_l * inner
            sum_ref[1, t] = felt_r * inner
        else:
            sum_ref[0, t] = sums_ref[0, t] + felt_l * inner
            sum_ref[1, t] = sums_ref[1, t] + felt_r * inner
        head = jnp.where(upper, other_ref[0, t], head) + c * jnp.where(upper, partner, inner)
        tail = jnp.where(upper, tail, other_ref[1, t]) + b * jnp.where(upper, inner, partner)
        if 4 << level == count:
            held_ref[t] = jnp.where(following, head, tail)
        else:
            held_ref[0, t] = head
            held_ref[1, t] = tail


def merge(level, held, coeffs, extra):
    count = lax.axis_size("rad")
    first = level == 0
    last = 4 << level == count
    sums = pltpu.VMEM(held.shape, f32)
    message = pltpu.VMEM(held.shape[1:] if last else held.shape, f32)
    return pl.pallas_call(
        functools.partial(merge_kernel, level, count, first),
        out_shape=[pltpu.VMEM(extra.shape, f32), message, sums] if first else [message, sums],
        in_specs=[VMEM] * 4,
        out_specs=[VMEM] * (3 if first else 2),
        input_output_aliases={3: 0} if first else {},
        cost_estimate=cost(40000),
        name="merge",
    )(*map(in_vmem, (held, swapped(held, "rad", 1 << level), coeffs, extra)))


def join_kernel(own_ref, other_ref, coeffs_ref, sums_ref, out_ref):
    tiles = own_ref.shape[0] - 1
    ghosts = []
    for e in range(2):
        for t in range(tiles + 1):
            value = (
                sums_ref[e, t]
                + coeffs_ref[2 * e] * other_ref[t]
                + coeffs_ref[2 * e + 1] * own_ref[t]
            )
            if t < tiles:
                out_ref[0, tiles * e + t] = value
            else:
                ghosts.append(value)
    out_ref[0, 2 * tiles] = ghosts[0] + pltpu.roll(ghosts[1], LANES // 2, 1)


def per_device(state, velocity, coupling, diffusivity, inverse, shifts):
    state = state[:, 0]
    fields, rows, cells = state.shape
    tiles = cells // LANES
    assert tiles == 2 and fields == 8 and 2 * rows <= LANES
    count = lax.axis_size("az")
    segments = lax.axis_size("rad")
    offsets, state_near, velocity, diffusivity, shifts, mixing = pl.pallas_call(
        offsets_kernel,
        out_shape=[
            pltpu.VMEM((2, tiles + 1, fields, LANES), f32),
            pltpu.VMEM(state.shape, f32),
            pltpu.VMEM((1, rows), f32),
            pltpu.VMEM((1, fields), f32),
            pltpu.SMEM(shifts.shape, jnp.int32),
            pltpu.SMEM(coupling.shape, f32),
        ],
        in_specs=[ANY] * 6,
        out_specs=[VMEM] * 4 + [SMEM] * 2,
        scratch_shapes=[
            pltpu.VMEM((fields, 8, rows), f32),
            pltpu.VMEM((fields, 8, rows), f32),
            pltpu.VMEM((fields, fields), f32),
            pltpu.SemaphoreType.DMA((8,)),
        ],
        cost_estimate=cost(5000),
        name="offsets",
    )(state, inverse, velocity[None], coupling, diffusivity[None], shifts)
    shifts = in_smem(shifts)
    spare = -(-count * 2 * rows // cells)
    solved, columns, coeffs, final = pl.pallas_call(
        functools.partial(solve_kernel, count, segments),
        out_shape=[
            pltpu.VMEM((rows + spare, tiles, fields, LANES), f32),
            pltpu.VMEM((2, rows, fields, LANES), f32),
            pltpu.VMEM((7 * log2(segments) - 7, fields, LANES), f32),
            pltpu.VMEM((4, fields, LANES), f32),
        ],
        in_specs=[SMEM] + [VMEM] * 4,
        out_specs=[VMEM] * 4,
        scratch_shapes=[
            pltpu.VMEM((fields, rows, cells), f32),
            pltpu.VMEM((fields * rows, cells + LANES), f32),
            pltpu.VMEM((fields * rows // LANES, fields * rows, LANES), f32),
        ],
        cost_estimate=cost(8000),
        name="solve",
    )(in_smem(mixing), *map(in_vmem, (state_near, velocity, diffusivity, inverse)))
    kept, held, sums = merge(0, offsets, coeffs, solved)
    bit = 1
    while 2 * bit < count:
        kept, coeffs = pl.pallas_call(
            functools.partial(select_kernel, bit),
            out_shape=[pltpu.VMEM(kept.shape, f32), pltpu.VMEM(coeffs.shape, f32)],
            in_specs=[SMEM] + [VMEM] * 3,
            out_specs=[VMEM] * 2,
            cost_estimate=cost(2800),
        name="select",
        )(shifts, in_vmem(kept), in_vmem(swapped(kept, "az", bit)), in_vmem(coeffs))
        bit *= 2
    rotated = pl.pallas_call(
        functools.partial(rotate_kernel, count, bit),
        out_shape=pltpu.VMEM((rows, tiles, fields, LANES), f32),
        in_specs=[SMEM] + [VMEM] * 2,
        out_specs=VMEM,
        scratch_shapes=[pltpu.VMEM((count * 2 * rows // LANES, fields, LANES), f32)],
        cost_estimate=cost(4000),
        name="rotate",
    )(shifts, in_vmem(kept), in_vmem(swapped(kept, "az", bit)))
    for level in range(1, log2(segments) - 1):
        held, sums = merge(level, held, coeffs, sums)
    forcing = pl.pallas_call(
        join_kernel,
        out_shape=pltpu.VMEM((1, 2 * tiles + 1, fields, LANES), f32),
        in_specs=[VMEM] * 4,
        out_specs=VMEM,
        cost_estimate=cost(400),
        name="join",
    )(*map(in_vmem, (held, swapped(held, "rad", segments // 2), final, sums)))
    parts = [forcing]
    bit = 1
    while bit < count:
        ours = parts[0] if len(parts) == 1 else jnp.concatenate(parts, 0)
        parts += [swapped(ours, "az", i * bit) for i in range(1, min(4, count // bit))]
        bit *= 4
    starts = [sum(x.shape[0] for x in parts[:i]) for i in range(len(parts))]
    out = pl.pallas_call(
        functools.partial(finish_kernel, count, starts),
        out_shape=jax.ShapeDtypeStruct(state.shape, f32),
        in_specs=[SMEM] + [VMEM] * (2 + len(parts)),
        out_specs=ANY,
        scratch_shapes=[
            pltpu.VMEM((count, 2, fields, LANES), f32),
            pltpu.VMEM((count, 2, tiles, fields, LANES), f32),
            pltpu.VMEM((rows // BATCH, tiles, BATCH * fields, LANES), f32),
            pltpu.SemaphoreType.DMA((rows // BATCH, tiles)),
        ],
        cost_estimate=cost(6000),
        name="finish",
    )(shifts, in_vmem(columns), in_vmem(rotated), *map(in_vmem, reversed(parts)))
    return out[:, None]


def solution(mesh):
    return jax.shard_map(
        per_device,
        mesh=mesh,
        in_specs=(P(None, None, "rad", "az"), P("rad"), P(), P(), P(), P("rad")),
        out_specs=P(None, None, "rad", "az"),
        check_vma=False,
    )
```
